32 devices in a mesh: gz: 8 (over z, x), gy: 4 (over y, core).
Axes of the slice: x: 2, y: 2, z: 4, core: 2. Of those that a mesh axis runs over, the one named last changes fastest.
Arguments:
- excess_warmth: float32 [384, 6144], P('gz', 'gy'), may hold values from -6 to 6
- pore_moisture: float32 [384, 6144], P('gz', 'gy'), may hold values from 0.55 to 1
- cement_maturity_degree: float32 [384, 6144], P('gz', 'gy'), may hold values from 0.05 to 0.85
- parcel_filled_tally: int32 [384, 48], P('gz', 'gy'), may hold values from 0 to 128
- parcel_keeper_position: int32 [384, 48], P('gz', 'gy'), may hold values from 0 to 1727, as said below
- layer_pouring_times: int32 [48], replicated, may hold values from 0 to 2000
- voigt_strains_stored: float32 [55296, 8, 128], P(('gz', 'gy')), may hold values from -4 to 4
- micro_tension: float32 [55296, 128], P(('gz', 'gy')), may hold values from 0.5 to 5
Outputs:
- temperature_new: float32 [384, 6144], P('gz', 'gy')
- humidity_new: float32 [384, 6144], P('gz', 'gy')
- cement_maturity_after: float32 [384, 6144], P('gz', 'gy')
- creep_strain: float32 [384, 6144], P('gz', 'gy')
- voigt_strains_after: float32 [55296, 8, 128], P(('gz', 'gy'))
- micro_tension_after: float32 [55296, 128], P(('gz', 'gy'))
The draws below stay inside these ranges and needn't reach their ends.
Inputs may be any that keep to these rules, and one draw needn't show every extreme that they name: `parcel_keeper_position`: number the devices gz index * 4 + gy index. The 576 blocks on one device carry distinct values; value // 54 is the device that holds the block's creep state. In every draw one device holds the states of exactly 54 blocks of every device.
All inputs are finite; a program needn't handle non-finite values.
Results may differ from the reference program's by a relative error of at most 0.00002.
Values sent between devices are 32-bit elements; how exact they have to be, the bound alone decides.
A program may use at most 64 MiB of HBM per device.

```python
import math
import jax
import jax.numpy as jnp
from jax import lax

CZ = 48
CY = 32
NX = 48
PARCEL_SITES = 128
KU = 8
SWEEPS = 3
LIFT = 8
VERTICAL_LINES = 384
LINE_SITES = 6144
PARCELS_PER_LINE = 48
NB = 576
CAP = 54
SLOTS = 1728
ALLSLOTS = 55296
NLIFT = 48
N_GZ = 8
N_GY = 4


def draw_parcel_keeper_position(key, part):
    sources = N_GZ * N_GY
    key_owner, key_perm, key_mix = jax.random.split(key, 3)
    forced = jax.random.randint(key_owner, (), 0, sources)

    def one_source(perm_key, mix_key):
        scores = jax.random.permutation(perm_key, SLOTS).astype(jnp.int32)
        slot_ids = jnp.arange(SLOTS).astype(jnp.int32)
        scores = jnp.where(slot_ids // CAP == forced, -1 - slot_ids % CAP, scores)
        ranking = jnp.argsort(scores, stable=True)[:NB].astype(jnp.int32)
        return ranking[jax.random.permutation(mix_key, NB)]
    chosen = jax.vmap(one_source)(jax.random.split(key_perm, sources), jax.random.split(key_mix, sources))
    layout = chosen.reshape(N_GZ, N_GY, CZ, NB // CZ).transpose(0, 2, 1, 3)
    return layout.reshape(VERTICAL_LINES, PARCELS_PER_LINE).astype(jnp.int32)


def with_ends(array, rng, low, top_value):
    longest = array.shape.index(max(array.shape))
    spots = []
    for shift in (0, 1):
        where = [jax.random.randint(jax.random.fold_in(rng, axis), (), 0, length) for axis, length in enumerate(array.shape)]
        where[longest] = (where[longest] + shift) % array.shape[longest]
        spots.append(tuple(where))
    return array.at[spots[0]].set(low).at[spots[1]].set(top_value)


def block_scale(stream_key, shape, cuts, smallest, largest):
    def one(dim, shards_of):
        draws = jax.random.uniform(jax.random.fold_in(jax.random.fold_in(stream_key, 6), dim), (shards_of,), jnp.float32, smallest / len(cuts), largest / len(cuts))
        return jnp.repeat(jnp.exp(draws), shape[dim] // shards_of).reshape((-1,) + (1,) * (len(shape) - dim - 1))

    factor_of = one(*cuts[0])
    for cut in cuts[1:]:
        factor_of = factor_of * one(*cut)
    return factor_of


def normal_values(stream_key, extent, spread, limit, cuts=(), held_as=jnp.bfloat16):
    level = block_scale(stream_key, extent, cuts, -0.22, 0.18) if cuts else 1.0
    values = jax.random.normal(stream_key, extent, jnp.float32) * spread * level
    return jnp.minimum(jnp.maximum(values, -limit), limit).astype(held_as)


def setup_inputs(seed: int = 0) -> dict:
    splits = jax.random.split(jax.random.key(seed), 9)
    return {
        "excess_warmth": normal_values(splits[0], (VERTICAL_LINES, LINE_SITES), 1.0, 6.0, ((0, 8), (1, 4)), jnp.float32),
        "pore_moisture": jnp.clip(0.55 + 0.45 * jax.random.uniform(splits[1], (VERTICAL_LINES, LINE_SITES), jnp.float32) ** block_scale(splits[1], (VERTICAL_LINES, LINE_SITES), ((0, 8), (1, 4)), -0.2, 0.2), 0.55, 1.0),
        "cement_maturity_degree": jnp.clip(0.05 + 0.8 * jax.random.uniform(splits[2], (VERTICAL_LINES, LINE_SITES), jnp.float32) ** block_scale(splits[2], (VERTICAL_LINES, LINE_SITES), ((0, 8), (1, 4)), -0.2, 0.2), 0.05, 0.85),
        "parcel_filled_tally": with_ends(jax.random.randint(splits[3], (VERTICAL_LINES, PARCELS_PER_LINE), 0, PARCEL_SITES + 1), jax.random.fold_in(splits[3], 1), 0, PARCEL_SITES).astype(jnp.int32),
        "parcel_keeper_position": draw_parcel_keeper_position(jax.random.fold_in(splits[8], 71), 0),
        "layer_pouring_times": with_ends(jax.random.randint(splits[5], (NLIFT,), 0, 2001), jax.random.fold_in(splits[5], 1), 0, 2000).astype(jnp.int32),
        "voigt_strains_stored": normal_values(splits[6], (ALLSLOTS, KU, PARCEL_SITES), 0.3, 4.0, ((0, 32),), jnp.float32),
        "micro_tension": jnp.clip(jnp.exp(math.log(5.0) - 2.3025851 * jax.random.uniform(splits[7], (ALLSLOTS, PARCEL_SITES), jnp.float32) ** block_scale(splits[7], (ALLSLOTS, PARCEL_SITES), ((0, 32),), -0.2, 0.2)), 0.5, 5.0),
    }


rate_base = 0.05
activation = 0.5
cement_warmth_output = 4.0
desiccation = 0.5
diff_floor = 0.05
humid_scale = 5.0
expansion_factor = 0.5
drying_contraction_factor = 2.0
now_hours = 2400.0
age_scale = 600.0
creep_activation = 0.3
kelvin_amp = 0.15
micro_rate = 0.2
flow_coef = 0.1

def cement_maturing_speed(field_temp, field_hum, degree):
    humid_term = 7.5 - 7.5 * field_hum
    humid_term = humid_term * humid_term
    return rate_base * (1.0 - degree) * jnp.exp(activation * field_temp) / (1.0 + humid_term * humid_term)

def diffusivity(field_hum):
    ratio = humid_scale * (1.0 - field_hum)
    power = ratio * ratio
    power = power * power
    power = power * power
    power = power * power
    return diff_floor + (1.0 - diff_floor) / (1.0 + power)

def smoothing_iteration(present_warmth, present_moisture, excess_warmth, pore_moisture, cement_maturity_degree, warmth_around, moisture_around):
    chemical_progress = cement_maturing_speed(present_warmth, present_moisture, cement_maturity_degree)
    emitted_warmth_total = warmth_around[0] + warmth_around[1] + warmth_around[2] + warmth_around[3] + warmth_around[4] + warmth_around[5]
    warmth_after = (excess_warmth + cement_warmth_output * chemical_progress + emitted_warmth_total) / 7.0
    own_diff = diffusivity(present_moisture)
    conduct = jnp.zeros_like(present_moisture)
    inflow = jnp.zeros_like(present_moisture)
    for neighbour in moisture_around:
        face_diff = 0.5 * (own_diff + diffusivity(neighbour))
        conduct = conduct + face_diff
        inflow = inflow + face_diff * neighbour
    moisture_after = (pore_moisture - desiccation * chemical_progress + inflow) / (1.0 + conduct)
    return (warmth_after, moisture_after)

def viscous_strain_advance(loading_tension, field_temp, field_hum, parcel_maturity, poured_tally, series_prior, micro_tension_before):
    factor = jnp.exp(creep_activation * field_temp) * (0.1 + 0.9 * field_hum * field_hum)
    lifetimes = 0.1 * 3.0 ** jnp.arange(series_prior.shape[-2]).astype(jnp.float32)
    decays = jnp.exp(-factor[..., None, :] / lifetimes[:, None])
    chain_new = decays * series_prior + kelvin_amp * (1.0 - decays) * loading_tension[..., None, :]
    solidify = jnp.sqrt(age_scale / parcel_maturity) + 0.2
    kelvin_part = solidify * lax.optimization_barrier(jnp.sum(chain_new - series_prior, axis=-2))
    prestress_next = micro_tension_before / (1.0 + micro_rate * factor * micro_tension_before)
    flow_part = flow_coef * factor * prestress_next * loading_tension
    position = jnp.arange(loading_tension.shape[-1]).astype(jnp.float32)
    placed = position < poured_tally
    series_result = jnp.where(placed[..., None, :], chain_new, series_prior)
    micro_tension_result = jnp.where(placed, prestress_next, micro_tension_before)
    small_change = jnp.where(placed, kelvin_part + flow_part, jnp.zeros_like(loading_tension))
    return (series_result, micro_tension_result, small_change)

def nearby_sites(values_in):
    col_total = values_in.shape[1]
    padded = jnp.pad(values_in, ((1, 1), (NX, NX)))
    upper_cell = padded[2:, NX:NX + col_total]
    lower_cell = padded[:-2, NX:NX + col_total]
    north_cell = padded[1:-1, 2 * NX:2 * NX + col_total]
    south_cell = padded[1:-1, 0:col_total]
    vertical_index = jnp.arange(col_total) % NX
    east_cell = jnp.where(vertical_index < NX - 1, padded[1:-1, NX + 1:NX + 1 + col_total], jnp.zeros_like(values_in))
    west_cell = jnp.where(vertical_index > 0, padded[1:-1, NX - 1:NX - 1 + col_total], jnp.zeros_like(values_in))
    return (upper_cell, lower_cell, north_cell, south_cell, east_cell, west_cell)

def reference(excess_warmth, pore_moisture, cement_maturity_degree, parcel_filled_tally, parcel_keeper_position, layer_pouring_times, voigt_strains_stored, micro_tension):
    present_warmth = excess_warmth
    present_moisture = pore_moisture
    for sweep_index in range(SWEEPS):
        present_warmth, present_moisture = smoothing_iteration(present_warmth, present_moisture, excess_warmth, pore_moisture, cement_maturity_degree, nearby_sites(present_warmth), nearby_sites(present_moisture))
    cement_maturity_after = cement_maturity_degree + cement_maturing_speed(present_warmth, present_moisture, cement_maturity_degree)
    loading_tension = -cement_maturity_after * (expansion_factor * present_warmth + drying_contraction_factor * (1.0 - present_moisture))
    row_ids = jnp.arange(VERTICAL_LINES).astype(jnp.int32)
    col_ids = jnp.arange(PARCELS_PER_LINE).astype(jnp.int32)
    sources = (row_ids[:, None] // CZ * N_GY + col_ids[None, :] // (CY * NX // PARCEL_SITES)).astype(jnp.int32)
    slot_index = (parcel_keeper_position // CAP * SLOTS + sources * CAP + parcel_keeper_position % CAP).astype(jnp.int32)
    flat_index = slot_index.reshape(-1)
    row_age = now_hours - layer_pouring_times.astype(jnp.float32)[row_ids // LIFT]
    parcel_maturity = jnp.broadcast_to(row_age[:, None, None], (VERTICAL_LINES, PARCELS_PER_LINE, 1))
    poured_tally = parcel_filled_tally.astype(jnp.float32)[..., None]
    series_prior = voigt_strains_stored[flat_index].reshape(VERTICAL_LINES, PARCELS_PER_LINE, KU, PARCEL_SITES)
    micro_tension_before = micro_tension[flat_index].reshape(VERTICAL_LINES, PARCELS_PER_LINE, PARCEL_SITES)
    series_result, micro_tension_result, small_change = viscous_strain_advance(loading_tension.reshape(VERTICAL_LINES, PARCELS_PER_LINE, PARCEL_SITES), present_warmth.reshape(VERTICAL_LINES, PARCELS_PER_LINE, PARCEL_SITES), present_moisture.reshape(VERTICAL_LINES, PARCELS_PER_LINE, PARCEL_SITES), parcel_maturity, poured_tally, series_prior, micro_tension_before)
    voigt_strains_after = voigt_strains_stored.at[flat_index].set(series_result.reshape(-1, KU, PARCEL_SITES))
    micro_tension_after = micro_tension.at[flat_index].set(micro_tension_result.reshape(-1, PARCEL_SITES))
    return (present_warmth, present_moisture, cement_maturity_after, small_change.reshape(VERTICAL_LINES, PARCELS_PER_LINE * PARCEL_SITES), voigt_strains_after, micro_tension_after)
```

```python
import functools

import jax
import jax.numpy as jnp
from jax import lax
from jax.experimental import pallas as pl
from jax.experimental.pallas import tpu as pltpu
from jax.sharding import PartitionSpec as P

NX = 48
SITES = 128
KU = 8
SWEEPS = 3
LIFT = 8
PAD = 128
TOP = 8
GROUP = 4
DRY = 0.05 + 0.95 / (1.0 + 5.0**16)
MESH = pl.DeviceIdType.MESH


def rate(temp, hum, degree):
    term = 7.5 - 7.5 * hum
    term = term * term
    return 0.05 * (1.0 - degree) * jnp.exp(0.5 * temp) / (1.0 + term * term)


def diffusivity(hum):
    ratio = 5.0 * (1.0 - hum)
    power = ratio * ratio
    power = power * power
    power = power * power
    power = power * power
    return 0.05 + 0.95 / (1.0 + power)


def padded_rows(count):
    return -(-count // 8) * 8


def greet_all(n, n_gy, me):
    barrier = pltpu.get_barrier_semaphore()

    def greet(j, carry):
        other = lax.rem(me + 1 + j, n)
        pl.semaphore_signal(
            barrier, inc=1, device_id=(other // n_gy, lax.rem(other, n_gy)), device_id_type=MESH
        )
        return carry

    lax.fori_loop(0, n - 1, greet, 0)
    pl.semaphore_wait(barrier, n - 1)


def partner(i, n, me):
    return lax.rem(me + 1 + lax.rem(i + n // 2 - 1, n - 1), n)


def sweep_and_send(
    n_gz, n_gy, cap,
    warmth, moisture, degree, tally, index, solid,
    temp_out, hum_out, degree_out, got,
    ext, diff, z_send, z_recv, blocks, send, z_sems, y_sems, out_sems, in_sems, own_sem,
):
    n = n_gz * n_gy
    rows, cols = warmth.shape
    wide = cols + 2 * PAD
    per_row = cols // SITES
    cp = padded_rows(cap + 1)
    gz = lax.axis_index("gz")
    gy = lax.axis_index("gy")
    me = gz * n_gy + gy
    greet_all(n, n_gy, me)

    x = lax.rem(lax.broadcasted_iota(jnp.int32, (8, cols), 1), NX)
    has_west = x > 0
    has_east = x < NX - 1
    inner = slice(PAD, PAD + cols)
    body_rows = slice(TOP, TOP + rows)

    ext[0, 0, body_rows, inner] = warmth[...]
    ext[0, 1, body_rows, inner] = moisture[...]

    for s in range(SWEEPS):
        for f in range(2):
            z_send[s, 0, f : f + 1] = ext[s, f, TOP : TOP + 1, inner]
            z_send[s, 1, f : f + 1] = ext[s, f, TOP + rows - 1 : TOP + rows, inner]

        def z_copy(side, s=s):
            to = gz - 1 + 2 * side
            return pltpu.make_async_remote_copy(
                src_ref=z_send.at[s, side],
                dst_ref=z_recv.at[s, 1 - side],
                send_sem=z_sems.at[s, 0, side],
                recv_sem=z_sems.at[s, 1, 1 - side],
                device_id=(to, gy),
                device_id_type=MESH,
            )

        def y_copy(side, s=s):
            to = gy - 1 + 2 * side
            a = PAD if side == 0 else cols
            b = PAD + cols if side == 0 else 0
            return pltpu.make_async_remote_copy(
                src_ref=ext.at[s, :, body_rows, pl.ds(a, PAD)],
                dst_ref=ext.at[s, :, body_rows, pl.ds(b, PAD)],
                send_sem=y_sems.at[s, 0, side],
                recv_sem=y_sems.at[s, 1, 1 - side],
                device_id=(gz, to),
                device_id_type=MESH,
            )

        there = (gz > 0, gz < n_gz - 1)
        beside = (gy > 0, gy < n_gy - 1)
        for side in range(2):
            pl.when(beside[side])(lambda side=side: y_copy(side).start())
            pl.when(there[side])(lambda side=side: z_copy(side).start())

        for side in range(2):

            @pl.when(jnp.logical_not(there[side]))
            def _(side=side, s=s):
                z_recv[s, side] = jnp.zeros((2, cols), jnp.float32)

            @pl.when(jnp.logical_not(beside[side]))
            def _(side=side, s=s):
                b = 0 if side == 0 else PAD + cols
                ext[s, :, body_rows, pl.ds(b, PAD)] = jnp.zeros((2, rows, PAD), jnp.float32)

        for side in range(2):
            pl.when(there[side])(lambda side=side: z_copy(1 - side).wait_recv())
            pl.when(beside[side])(lambda side=side: y_copy(1 - side).wait_recv())

        for f in range(2):
            ext[s, f, TOP - 1 : TOP, inner] = z_recv[s, 0, f : f + 1]
            ext[s, f, TOP + rows : TOP + rows + 1, inner] = z_recv[s, 1, f : f + 1]
        diff[TOP - 1 : TOP, inner] = diffusivity(z_recv[s, 0, 1:2])
        diff[TOP + rows : TOP + rows + 1, inner] = diffusivity(z_recv[s, 1, 1:2])
        for r in range(0, rows, 8):
            here = slice(TOP + r, TOP + r + 8)
            diff[here, :] = diffusivity(ext[s, 1, here, :])

        for r in range(0, rows, 8):
            here = slice(TOP + r, TOP + r + 8)
            up = slice(TOP + r + 1, TOP + r + 9)
            down = slice(TOP + r - 1, TOP + r + 7)
            own = slice(r, r + 8)
            temp = ext[s, 0, here, :]
            hum = ext[s, 1, here, :]
            cond = diff[here, :]

            def aside(v, shift):
                return pltpu.roll(v, shift % wide, 1)[:, inner]

            total = (
                ext[s, 0, up, inner] + ext[s, 0, down, inner] + aside(temp, -NX) + aside(temp, NX)
            )
            total = total + jnp.where(has_east, aside(temp, -1), 0.0)
            total = total + jnp.where(has_west, aside(temp, 1), 0.0)
            t0 = temp[:, inner]
            h0 = hum[:, inner]
            d0 = cond[:, inner]
            progress = rate(t0, h0, degree[own, :])
            near = [
                (ext[s, 1, up, inner], diff[up, inner]),
                (ext[s, 1, down, inner], diff[down, inner]),
                (aside(hum, -NX), aside(cond, -NX)),
                (aside(hum, NX), aside(cond, NX)),
                (
                    jnp.where(has_east, aside(hum, -1), 0.0),
                    jnp.where(has_east, aside(cond, -1), DRY),
                ),
                (
                    jnp.where(has_west, aside(hum, 1), 0.0),
                    jnp.where(has_west, aside(cond, 1), DRY),
                ),
            ]
            conduct = None
            inflow = None
            for g, dg in near:
                c = 0.5 * (d0 + dg)
                conduct = c if conduct is None else conduct + c
                inflow = c * g if inflow is None else inflow + c * g
            t1 = (warmth[own, :] + 4.0 * progress + total) / 7.0
            h1 = (moisture[own, :] - 0.5 * progress + inflow) / (1.0 + conduct)
            if s < SWEEPS - 1:
                ext[s + 1, 0, here, inner] = t1
                ext[s + 1, 1, here, inner] = h1
            else:
                temp_out[own, :] = t1
                hum_out[own, :] = h1
                a1 = degree[own, :] + rate(t1, h1, degree[own, :])
                degree_out[own, :] = a1
                stress = -a1 * (0.5 * t1 + 2.0 * (1.0 - h1))
                phi = jnp.exp(0.3 * t1) * (0.1 + 0.9 * h1 * h1)
                lane = lax.broadcasted_iota(jnp.int32, (8, SITES), 1)
                for j in range(per_row):
                    cut = slice(j * SITES, (j + 1) * SITES)
                    at = slice(j * rows + r, j * rows + r + 8)
                    placed = lane < tally[own, j : j + 1]
                    blocks[0, at, :] = jnp.where(placed, phi[:, cut], 0.0)
                    blocks[1, at, :] = jnp.where(placed, stress[:, cut], 0.0)

    nb = rows * per_row
    blocks[0, nb : nb + 8, :] = jnp.zeros((8, SITES), jnp.float32)
    blocks[1, nb : nb + 8, :] = jnp.zeros((8, SITES), jnp.float32)

    def copy_to(i, o):
        return pltpu.make_async_remote_copy(
            src_ref=send.at[o],
            dst_ref=got.at[me],
            send_sem=out_sems.at[o],
            recv_sem=in_sems.at[me],
            device_id=(o // n_gy, lax.rem(o, n_gy)),
            device_id_type=MESH,
        )

    def fill(o):
        for l in range(cap):
            k = index[o * cap + l]
            send[o, l : l + 1, :] = blocks[0, pl.ds(k, 1), :]
            send[o, cp + l : cp + l + 1, :] = blocks[1, pl.ds(k, 1), :]
        send[o, cap : cap + 1, :] = solid[pl.ds(o, 1), :]

    def push(i, carry):
        o = partner(i, n, me)
        fill(o)
        copy_to(i, o).start()
        return carry

    lax.fori_loop(0, n - 1, push, 0)
    fill(me)
    own_copy = pltpu.make_async_copy(send.at[me], got.at[me], own_sem)
    own_copy.start()

    for s in range(SWEEPS):
        for side in range(2):
            a = PAD if side == 0 else cols
            pl.when((gz > 0, gz < n_gz - 1)[side])(
                lambda s=s, side=side: pltpu.make_async_remote_copy(
                    src_ref=z_send.at[s, side],
                    dst_ref=z_recv.at[s, 1 - side],
                    send_sem=z_sems.at[s, 0, side],
                    recv_sem=z_sems.at[s, 1, 1 - side],
                    device_id=(gz - 1 + 2 * side, gy),
                    device_id_type=MESH,
                ).wait_send()
            )
            pl.when((gy > 0, gy < n_gy - 1)[side])(
                lambda s=s, side=side, a=a: pltpu.make_async_remote_copy(
                    src_ref=ext.at[s, :, body_rows, pl.ds(a, PAD)],
                    dst_ref=ext.at[s, :, body_rows, pl.ds(a, PAD)],
                    send_sem=y_sems.at[s, 0, side],
                    recv_sem=y_sems.at[s, 1, 1 - side],
                    device_id=(gz, gy - 1 + 2 * side),
                    device_id_type=MESH,
                ).wait_send()
            )

    own_copy.wait()

    def finish(i, carry):
        o = partner(i, n, me)
        pltpu.make_async_remote_copy(
            src_ref=send.at[o],
            dst_ref=got.at[o],
            send_sem=out_sems.at[o],
            recv_sem=in_sems.at[o],
            device_id=(o // n_gy, lax.rem(o, n_gy)),
            device_id_type=MESH,
        ).wait()
        return carry

    lax.fori_loop(0, n - 1, finish, 0)


def creep(cap, got, chain, micro, chain_out, micro_out, change):
    cp = padded_rows(cap + 1)
    unit = lax.broadcasted_iota(jnp.int32, (KU, SITES), 0)
    speed = jnp.full((KU, SITES), -10.0, jnp.float32)
    for m in range(1, KU):
        speed = jnp.where(unit == m, -10.0 / 3.0**m, speed)
    sub = lax.broadcasted_iota(jnp.int32, (cap, SITES), 0)
    lane = lax.broadcasted_iota(jnp.int32, (cap, SITES), 1)
    for q in range(GROUP):
        base = q * cap
        phi = got[q, 0:cap, :]
        stress = got[q, cp : cp + cap, :]
        row = got[q, cap : cap + 1, :]
        solid = jnp.sum(jnp.where(sub == lane, row, 0.0), axis=1, keepdims=True)
        s0 = micro[base : base + cap, :]
        s1 = s0 / (1.0 + 0.2 * phi * s0)
        micro_out[base : base + cap, :] = s1
        flow = 0.1 * phi * s1 * stress
        for l0 in range(0, cap, 8):
            l1 = min(l0 + 8, cap)
            old = chain[base + l0 : base + l1]
            decay = jnp.exp(phi[l0:l1][:, None, :] * speed[None])
            new = decay * old + 0.15 * (1.0 - decay) * stress[l0:l1][:, None, :]
            chain_out[base + l0 : base + l1] = new
            kelvin = jnp.sum(new - old, axis=1)
            change[q, l0:l1, :] = solid[l0:l1] * kelvin + flow[l0:l1]
        change[q, cap:cp, :] = jnp.zeros((cp - cap, SITES), jnp.float32)


def send_back(n_gz, n_gy, change, where, out, back, out_sems, in_sems):
    n = n_gz * n_gy
    rows, cols = out.shape
    cp = change.shape[1]
    me = lax.axis_index("gz") * n_gy + lax.axis_index("gy")
    greet_all(n, n_gy, me)

    def push(i, carry):
        o = partner(i, n, me)
        pltpu.make_async_remote_copy(
            src_ref=change.at[o],
            dst_ref=back.at[pl.ds(pl.multiple_of(me * cp, 8), cp)],
            send_sem=out_sems.at[o],
            recv_sem=in_sems.at[me],
            device_id=(o // n_gy, lax.rem(o, n_gy)),
            device_id_type=MESH,
        ).start()
        return carry

    lax.fori_loop(0, n - 1, push, 0)
    back[pl.ds(pl.multiple_of(me * cp, 8), cp), :] = change[me]

    def finish(i, carry):
        o = partner(i, n, me)
        pltpu.make_async_remote_copy(
            src_ref=change.at[o],
            dst_ref=back.at[pl.ds(pl.multiple_of(o * cp, 8), cp)],
            send_sem=out_sems.at[o],
            recv_sem=in_sems.at[o],
            device_id=(o // n_gy, lax.rem(o, n_gy)),
            device_id_type=MESH,
        ).wait()
        return carry

    lax.fori_loop(0, n - 1, finish, 0)
    per_row = cols // SITES

    def place(g, carry):
        r = pl.multiple_of(g * 8, 8)
        for j in range(per_row):
            lines = [back[pl.ds(where[(r + k) * per_row + j], 1), :] for k in range(8)]
            out[pl.ds(r, 8), j * SITES : (j + 1) * SITES] = jnp.concatenate(lines, axis=0)
        return carry

    lax.fori_loop(0, rows // 8, place, 0)


def body(n_gz, n_gy, warmth, moisture, degree, tally, keeper, pouring, chain, micro):
    n = n_gz * n_gy
    rows, cols = warmth.shape
    per_row = cols // SITES
    slots = chain.shape[0]
    cap = slots // n
    cp = padded_rows(cap + 1)
    nb = rows * per_row
    lifts = rows // LIFT
    vm = pl.BlockSpec(memory_space=pltpu.VMEM)
    sm = pl.BlockSpec(memory_space=pltpu.SMEM)
    hbm = pl.BlockSpec(memory_space=pl.ANY)
    f32 = jnp.float32

    local_times = lax.dynamic_slice_in_dim(pouring, lax.axis_index("gz") * lifts, lifts)
    age = 2400.0 - jnp.repeat(local_times, LIFT).astype(f32)
    solid = jnp.sqrt(600.0 / age) + 0.2
    flat = keeper.reshape(-1)
    hit = flat[None, :] == jnp.arange(slots, dtype=jnp.int32)[:, None]
    block = jnp.arange(nb, dtype=jnp.int32)
    held = (block % per_row) * rows + block // per_row
    index = nb + jnp.sum(jnp.where(hit, held[None, :] - nb, 0), axis=1)
    solid_slot = jnp.sum(jnp.where(hit, jnp.repeat(solid, per_row)[None, :], 0.0), axis=1)
    solid_rows = jnp.pad(solid_slot.reshape(n, cap), ((0, 0), (0, SITES - cap)))
    where = (flat // cap) * cp + flat % cap

    field = jax.ShapeDtypeStruct((rows, cols), f32)
    temp, hum, degree_after, got = pl.pallas_call(
        functools.partial(sweep_and_send, n_gz, n_gy, cap),
        out_shape=(field, field, field, jax.ShapeDtypeStruct((n, 2 * cp, SITES), f32)),
        in_specs=[vm, vm, vm, vm, sm, vm],
        out_specs=(vm, vm, vm, hbm),
        scratch_shapes=[
            pltpu.VMEM((SWEEPS, 2, rows + 2 * TOP, cols + 2 * PAD), f32),
            pltpu.VMEM((rows + 2 * TOP, cols + 2 * PAD), f32),
            pltpu.VMEM((SWEEPS, 2, 2, cols), f32),
            pltpu.VMEM((SWEEPS, 2, 2, cols), f32),
            pltpu.VMEM((2, nb + 8, SITES), f32),
            pltpu.VMEM((n, 2 * cp, SITES), f32),
            pltpu.SemaphoreType.DMA((SWEEPS, 2, 2)),
            pltpu.SemaphoreType.DMA((SWEEPS, 2, 2)),
            pltpu.SemaphoreType.DMA((n,)),
            pltpu.SemaphoreType.DMA((n,)),
            pltpu.SemaphoreType.DMA,
        ],
        compiler_params=pltpu.CompilerParams(
            collective_id=0, has_side_effects=True, vmem_limit_bytes=40 * 1024 * 1024
        ),
        name="sweep_and_send",
    )(warmth, moisture, degree, tally, index, solid_rows)

    chain_after, micro_after, change = pl.pallas_call(
        functools.partial(creep, cap),
        grid=(n // GROUP,),
        out_shape=(
            jax.ShapeDtypeStruct(chain.shape, f32),
            jax.ShapeDtypeStruct(micro.shape, f32),
            jax.ShapeDtypeStruct((n, cp, SITES), f32),
        ),
        in_specs=[
            pl.BlockSpec((GROUP, 2 * cp, SITES), lambda i: (i, 0, 0)),
            pl.BlockSpec((GROUP * cap, KU, SITES), lambda i: (i, 0, 0)),
            pl.BlockSpec((GROUP * cap, SITES), lambda i: (i, 0)),
        ],
        out_specs=(
            pl.BlockSpec((GROUP * cap, KU, SITES), lambda i: (i, 0, 0)),
            pl.BlockSpec((GROUP * cap, SITES), lambda i: (i, 0)),
            pl.BlockSpec((GROUP, cp, SITES), lambda i: (i, 0, 0)),
        ),
        compiler_params=pltpu.CompilerParams(vmem_limit_bytes=40 * 1024 * 1024),
        name="creep",
    )(got, chain, micro)

    creep_cells = pl.pallas_call(
        functools.partial(send_back, n_gz, n_gy),
        out_shape=field,
        in_specs=[vm, sm],
        out_specs=vm,
        scratch_shapes=[
            pltpu.VMEM((n * cp, SITES), f32),
            pltpu.SemaphoreType.DMA((n,)),
            pltpu.SemaphoreType.DMA((n,)),
        ],
        compiler_params=pltpu.CompilerParams(
            collective_id=1, has_side_effects=True, vmem_limit_bytes=40 * 1024 * 1024
        ),
        name="send_back",
    )(change, where)
    return temp, hum, degree_after, creep_cells, chain_after, micro_after


def solution(mesh):
    n_gz, n_gy = mesh.shape["gz"], mesh.shape["gy"]
    cells = P("gz", "gy")
    states = P(("gz", "gy"), None, None)
    tension = P(("gz", "gy"), None)
    return jax.shard_map(
        functools.partial(body, n_gz, n_gy),
        mesh=mesh,
        in_specs=(cells, cells, cells, cells, cells, P(), states, tension),
        out_specs=(cells, cells, cells, cells, states, tension),
        check_vma=False,
    )
```

```python
import functools

import jax
import jax.numpy as jnp
from jax import lax
from jax.experimental import pallas as pl
from jax.experimental.pallas import tpu as pltpu
from jax.sharding import PartitionSpec as P

NX = 48
SITES = 128
KU = 8
SWEEPS = 3
LIFT = 8
PAD = 128
TOP = 8
GROUP = 4
DIRECT = 24
SPILL = 40
DRY = 0.05 + 0.95 / (1.0 + 5.0**16)
MESH = pl.DeviceIdType.MESH


def rate(temp, hum, degree):
    term = 7.5 - 7.5 * hum
    term = term * term
    return 0.05 * (1.0 - degree) * jnp.exp(0.5 * temp) / (1.0 + term * term)


def diffusivity(hum):
    ratio = 5.0 * (1.0 - hum)
    power = ratio * ratio
    power = power * power
    power = power * power
    power = power * power
    return 0.05 + 0.95 / (1.0 + power)


def padded_rows(count):
    return -(-count // 8) * 8


def greet_all(n, n_gy, me):
    barrier = pltpu.get_barrier_semaphore()

    def greet(j, carry):
        other = lax.rem(me + 1 + j, n)
        pl.semaphore_signal(
            barrier, inc=1, device_id=(other // n_gy, lax.rem(other, n_gy)), device_id_type=MESH
        )
        return carry

    lax.fori_loop(0, n - 1, greet, 0)
    pl.semaphore_wait(barrier, n - 1)


def partner(i, n, me):
    return lax.rem(me + 1 + lax.rem(i + n // 2 - 1, n - 1), n)


def sweep_and_send(
    n_gz, n_gy, lean,
    warmth, moisture, degree, tally, index, spill_index, notes,
    temp_out, hum_out, degree_out, blocks, notes_in, *rest,
):
    if lean:
        got, got_spill = rest[:2]
        rest = rest[2:]
    ext, diff, z_send, z_recv, z_sems, y_sems, note_out, note_in = rest[:8]
    if lean:
        send, out_sems, in_sems, own_sems, relay_out, relay_in = rest[8:]
    n = n_gz * n_gy
    rows, cols = warmth.shape
    wide = cols + 2 * PAD
    per_row = cols // SITES
    gz = lax.axis_index("gz")
    gy = lax.axis_index("gy")
    me = gz * n_gy + gy
    greet_all(n, n_gy, me)

    def note_copy(o, at):
        return pltpu.make_async_remote_copy(
            src_ref=notes.at[o],
            dst_ref=notes_in.at[at],
            send_sem=note_out.at[o],
            recv_sem=note_in.at[at],
            device_id=(o // n_gy, lax.rem(o, n_gy)),
            device_id_type=MESH,
        )

    def tell(i, carry):
        note_copy(partner(i, n, me), me).start()
        return carry

    x = lax.rem(lax.broadcasted_iota(jnp.int32, (8, cols), 1), NX)
    has_west = x > 0
    has_east = x < NX - 1
    inner = slice(PAD, PAD + cols)
    body_rows = slice(TOP, TOP + rows)

    ext[0, 0, body_rows, inner] = warmth[...]
    ext[0, 1, body_rows, inner] = moisture[...]

    for s in range(SWEEPS):
        for f in range(2):
            z_send[s, 0, f : f + 1] = ext[s, f, TOP : TOP + 1, inner]
            z_send[s, 1, f : f + 1] = ext[s, f, TOP + rows - 1 : TOP + rows, inner]

        def z_copy(side, s=s):
            to = gz - 1 + 2 * side
            return pltpu.make_async_remote_copy(
                src_ref=z_send.at[s, side],
                dst_ref=z_recv.at[s, 1 - side],
                send_sem=z_sems.at[s, 0, side],
                recv_sem=z_sems.at[s, 1, 1 - side],
                device_id=(to, gy),
                device_id_type=MESH,
            )

        def y_copy(side, s=s):
            to = gy - 1 + 2 * side
            a = PAD if side == 0 else cols
            b = PAD + cols if side == 0 else 0
            return pltpu.make_async_remote_copy(
                src_ref=ext.at[s, :, body_rows, pl.ds(a, PAD)],
                dst_ref=ext.at[s, :, body_rows, pl.ds(b, PAD)],
                send_sem=y_sems.at[s, 0, side],
                recv_sem=y_sems.at[s, 1, 1 - side],
                device_id=(gz, to),
                device_id_type=MESH,
            )

        there = (gz > 0, gz < n_gz - 1)
        beside = (gy > 0, gy < n_gy - 1)
        for side in range(2):
            pl.when(beside[side])(lambda side=side: y_copy(side).start())
            pl.when(there[side])(lambda side=side: z_copy(side).start())

        if s == 0:
            lax.fori_loop(0, n - 1, tell, 0)
            notes_in[me] = notes[me]

        for side in range(2):

            @pl.when(jnp.logical_not(there[side]))
            def _(side=side, s=s):
                z_recv[s, side] = jnp.zeros((2, cols), jnp.float32)

            @pl.when(jnp.logical_not(beside[side]))
            def _(side=side, s=s):
                b = 0 if side == 0 else PAD + cols
                ext[s, :, body_rows, pl.ds(b, PAD)] = jnp.zeros((2, rows, PAD), jnp.float32)

        for side in range(2):
            pl.when(there[side])(lambda side=side: z_copy(1 - side).wait_recv())
            pl.when(beside[side])(lambda side=side: y_copy(1 - side).wait_recv())

        for f in range(2):
            ext[s, f, TOP - 1 : TOP, inner] = z_recv[s, 0, f : f + 1]
            ext[s, f, TOP + rows : TOP + rows + 1, inner] = z_recv[s, 1, f : f + 1]
        diff[TOP - 1 : TOP, inner] = diffusivity(z_recv[s, 0, 1:2])
        diff[TOP + rows : TOP + rows + 1, inner] = diffusivity(z_recv[s, 1, 1:2])
        for r in range(0, rows, 8):
            here = slice(TOP + r, TOP + r + 8)
            diff[here, :] = diffusivity(ext[s, 1, here, :])

        for r in range(0, rows, 8):
            here = slice(TOP + r, TOP + r + 8)
            up = slice(TOP + r + 1, TOP + r + 9)
            down = slice(TOP + r - 1, TOP + r + 7)
            own = slice(r, r + 8)
            temp = ext[s, 0, here, :]
            hum = ext[s, 1, here, :]
            cond = diff[here, :]

            def aside(v, shift):
                return pltpu.roll(v, shift % wide, 1)[:, inner]

            total = (
                ext[s, 0, up, inner] + ext[s, 0, down, inner] + aside(temp, -NX) + aside(temp, NX)
            )
            total = total + jnp.where(has_east, aside(temp, -1), 0.0)
            total = total + jnp.where(has_west, aside(temp, 1), 0.0)
            t0 = temp[:, inner]
            h0 = hum[:, inner]
            d0 = cond[:, inner]
            progress = rate(t0, h0, degree[own, :])
            near = [
                (ext[s, 1, up, inner], diff[up, inner]),
                (ext[s, 1, down, inner], diff[down, inner]),
                (aside(hum, -NX), aside(cond, -NX)),
                (aside(hum, NX), aside(cond, NX)),
                (
                    jnp.where(has_east, aside(hum, -1), 0.0),
                    jnp.where(has_east, aside(cond, -1), DRY),
                ),
                (
                    jnp.where(has_west, aside(hum, 1), 0.0),
                    jnp.where(has_west, aside(cond, 1), DRY),
                ),
            ]
            conduct = None
            inflow = None
            for g, dg in near:
                c = 0.5 * (d0 + dg)
                conduct = c if conduct is None else conduct + c
                inflow = c * g if inflow is None else inflow + c * g
            t1 = (warmth[own, :] + 4.0 * progress + total) / 7.0
            h1 = (moisture[own, :] - 0.5 * progress + inflow) / (1.0 + conduct)
            if s < SWEEPS - 1:
                ext[s + 1, 0, here, inner] = t1
                ext[s + 1, 1, here, inner] = h1
            else:
                temp_out[own, :] = t1
                hum_out[own, :] = h1
                a1 = degree[own, :] + rate(t1, h1, degree[own, :])
                degree_out[own, :] = a1
                stress = -a1 * (0.5 * t1 + 2.0 * (1.0 - h1))
                phi = jnp.exp(0.3 * t1) * (0.1 + 0.9 * h1 * h1)
                lane = lax.broadcasted_iota(jnp.int32, (8, SITES), 1)
                for j in range(per_row):
                    cut = slice(j * SITES, (j + 1) * SITES)
                    at = slice(j * rows + r, j * rows + r + 8)
                    placed = lane < tally[own, j : j + 1]
                    blocks[0, at, :] = jnp.where(placed, phi[:, cut], 0.0)
                    blocks[1, at, :] = jnp.where(placed, stress[:, cut], 0.0)

    nb = rows * per_row
    blocks[0, nb : nb + 8, :] = jnp.zeros((8, SITES), jnp.float32)
    blocks[1, nb : nb + 8, :] = jnp.zeros((8, SITES), jnp.float32)

    if lean:
        z, x = gz // 2, lax.rem(gz, 2)
        y, core = gy // 2, lax.rem(gy, 2)
        depth = n // 8

        def spill_copy(sem, arrived, base, count, to):
            part = got_spill.at[pl.ds(base, count)]
            return pltpu.make_async_remote_copy(
                src_ref=part,
                dst_ref=part,
                send_sem=relay_out.at[sem],
                recv_sem=relay_in.at[arrived],
                device_id=to,
                device_id_type=MESH,
            )

        line = (core * 4 + x * 2 + y) * depth
        for l in range(SPILL):
            k = spill_index[l]
            got_spill[line + z, l : l + 1, :] = blocks[0, pl.ds(k, 1), :]
            got_spill[line + z, SPILL + l : SPILL + l + 1, :] = blocks[1, pl.ds(k, 1), :]

        def z_other(d):
            return lax.rem(z + d, depth)

        for d in range(1, depth):
            spill_copy(d, depth - d, line + z, 1, (z_other(d) * 2 + x, gy)).start()

        def fill(o):
            for l in range(DIRECT):
                k = index[o * DIRECT + l]
                send[o, l : l + 1, :] = blocks[0, pl.ds(k, 1), :]
                send[o, DIRECT + l : DIRECT + l + 1, :] = blocks[1, pl.ds(k, 1), :]

        def row_copy(o, at):
            return pltpu.make_async_remote_copy(
                src_ref=send.at[o],
                dst_ref=got.at[at],
                send_sem=out_sems.at[o],
                recv_sem=in_sems.at[at],
                device_id=(o // n_gy, lax.rem(o, n_gy)),
                device_id_type=MESH,
            )

        def push(i, carry):
            o = partner(i, n, me)
            fill(o)
            row_copy(o, me).start()
            return carry

        lax.fori_loop(0, n - 1, push, 0)
        fill(me)
        own_copy = pltpu.make_async_copy(send.at[me], got.at[me], own_sems)
        own_copy.start()

        for d in range(1, depth):
            spill_copy(d, depth - d, line + z_other(d), 1, (z_other(d) * 2 + x, gy)).wait_recv()
        spill_copy(depth, depth, line, depth, (gz, (1 - y) * 2 + core)).start()
        other = (core * 4 + x * 2 + 1 - y) * depth
        spill_copy(depth, depth, other, depth, (gz, (1 - y) * 2 + core)).wait_recv()
        pair = (core * 4 + x * 2) * depth
        spill_copy(depth + 1, depth + 1, pair, 2 * depth, (z * 2 + 1 - x, gy)).start()
        other = (core * 4 + (1 - x) * 2) * depth
        spill_copy(depth + 1, depth + 1, other, 2 * depth, (z * 2 + 1 - x, gy)).wait_recv()
        half = core * 4 * depth
        spill_copy(depth + 2, depth + 2, half, 4 * depth, (gz, y * 2 + 1 - core)).start()
        other = (1 - core) * 4 * depth
        spill_copy(depth + 2, depth + 2, other, 4 * depth, (gz, y * 2 + 1 - core)).wait_recv()

        for d in range(1, depth):
            spill_copy(d, depth - d, line + z, 1, (z_other(d) * 2 + x, gy)).wait_send()
        spill_copy(depth, depth, line, depth, (gz, (1 - y) * 2 + core)).wait_send()
        spill_copy(depth + 1, depth + 1, pair, 2 * depth, (z * 2 + 1 - x, gy)).wait_send()
        spill_copy(depth + 2, depth + 2, half, 4 * depth, (gz, y * 2 + 1 - core)).wait_send()

    for s in range(SWEEPS):
        for side in range(2):
            a = PAD if side == 0 else cols
            pl.when((gz > 0, gz < n_gz - 1)[side])(
                lambda s=s, side=side: pltpu.make_async_remote_copy(
                    src_ref=z_send.at[s, side],
                    dst_ref=z_recv.at[s, 1 - side],
                    send_sem=z_sems.at[s, 0, side],
                    recv_sem=z_sems.at[s, 1, 1 - side],
                    device_id=(gz - 1 + 2 * side, gy),
                    device_id_type=MESH,
                ).wait_send()
            )
            pl.when((gy > 0, gy < n_gy - 1)[side])(
                lambda s=s, side=side, a=a: pltpu.make_async_remote_copy(
                    src_ref=ext.at[s, :, body_rows, pl.ds(a, PAD)],
                    dst_ref=ext.at[s, :, body_rows, pl.ds(a, PAD)],
                    send_sem=y_sems.at[s, 0, side],
                    recv_sem=y_sems.at[s, 1, 1 - side],
                    device_id=(gz, gy - 1 + 2 * side),
                    device_id_type=MESH,
                ).wait_send()
            )

    def told(i, carry):
        o = partner(i, n, me)
        note_copy(o, o).wait()
        return carry

    lax.fori_loop(0, n - 1, told, 0)

    if lean:
        own_copy.wait()

        def finish(i, carry):
            o = partner(i, n, me)
            row_copy(o, o).wait()
            return carry

        lax.fori_loop(0, n - 1, finish, 0)


def send_dense(
    n_gz, n_gy, cap, blocks, index, solid, got, send, out_sems, in_sems, own_sem
):
    n = n_gz * n_gy
    cp = padded_rows(cap + 1)
    me = lax.axis_index("gz") * n_gy + lax.axis_index("gy")
    greet_all(n, n_gy, me)

    def row_copy(o, at):
        return pltpu.make_async_remote_copy(
            src_ref=send.at[o],
            dst_ref=got.at[at],
            send_sem=out_sems.at[o],
            recv_sem=in_sems.at[at],
            device_id=(o // n_gy, lax.rem(o, n_gy)),
            device_id_type=MESH,
        )

    def fill(o):
        for l in range(cap):
            k = index[o * cap + l]
            send[o, l : l + 1, :] = blocks[0, pl.ds(k, 1), :]
            send[o, cp + l : cp + l + 1, :] = blocks[1, pl.ds(k, 1), :]
        send[o, cap : cap + 1, :] = solid[pl.ds(o, 1), :]

    def push(i, carry):
        o = partner(i, n, me)
        fill(o)
        row_copy(o, me).start()
        return carry

    lax.fori_loop(0, n - 1, push, 0)
    fill(me)
    own_copy = pltpu.make_async_copy(send.at[me], got.at[me], own_sem)
    own_copy.start()
    own_copy.wait()

    def finish(i, carry):
        o = partner(i, n, me)
        row_copy(o, o).wait()
        return carry

    lax.fori_loop(0, n - 1, finish, 0)


def creep(cap, got, chain, micro, chain_out, micro_out, change):
    cp = padded_rows(cap + 1)
    unit = lax.broadcasted_iota(jnp.int32, (KU, SITES), 0)
    speed = jnp.full((KU, SITES), -10.0, jnp.float32)
    for m in range(1, KU):
        speed = jnp.where(unit == m, -10.0 / 3.0**m, speed)
    sub = lax.broadcasted_iota(jnp.int32, (cap, SITES), 0)
    lane = lax.broadcasted_iota(jnp.int32, (cap, SITES), 1)
    for q in range(GROUP):
        base = q * cap
        phi = got[q, 0:cap, :]
        stress = got[q, cp : cp + cap, :]
        row = got[q, cap : cap + 1, :]
        solid = jnp.sum(jnp.where(sub == lane, row, 0.0), axis=1, keepdims=True)
        s0 = micro[base : base + cap, :]
        s1 = s0 / (1.0 + 0.2 * phi * s0)
        micro_out[base : base + cap, :] = s1
        flow = 0.1 * phi * s1 * stress
        for l0 in range(0, cap, 8):
            l1 = min(l0 + 8, cap)
            old = chain[base + l0 : base + l1]
            decay = jnp.exp(phi[l0:l1][:, None, :] * speed[None])
            new = decay * old + 0.15 * (1.0 - decay) * stress[l0:l1][:, None, :]
            chain_out[base + l0 : base + l1] = new
            kelvin = jnp.sum(new - old, axis=1)
            change[q, l0:l1, :] = solid[l0:l1] * kelvin + flow[l0:l1]
        change[q, cap:cp, :] = jnp.zeros((cp - cap, SITES), jnp.float32)


def creep_lean(cap, depth, got, spill, notes, chain, micro, chain_out, micro_out, change, change_spill):
    held = DIRECT + SPILL
    unit = lax.broadcasted_iota(jnp.int32, (KU, SITES), 0)
    speed = jnp.full((KU, SITES), -10.0, jnp.float32)
    for m in range(1, KU):
        speed = jnp.where(unit == m, -10.0 / 3.0**m, speed)
    sub = lax.broadcasted_iota(jnp.int32, (cap, SITES), 0)
    lane = lax.broadcasted_iota(jnp.int32, (cap, SITES), 1)
    row_id = lax.broadcasted_iota(jnp.int32, (cap, held), 1).astype(jnp.float32)
    exact = lax.Precision.HIGHEST
    for q in range(GROUP):
        base = q * cap
        source = pl.program_id(0) * GROUP + q
        z, x = source // 8, lax.rem(source, 8) // 4
        y, core = lax.rem(source, 4) // 2, lax.rem(source, 2)
        place = (core * 4 + x * 2 + y) * depth + z

        def column(r):
            row = notes[q, r : r + 1, :]
            return jnp.sum(jnp.where(sub == lane, row, 0.0), axis=1, keepdims=True)

        pick = (column(0) == row_id).astype(jnp.float32)
        solid = column(1)
        rows_phi = jnp.concatenate([got[q, 0:DIRECT, :], spill[place, 0:SPILL, :]], axis=0)
        rows_stress = jnp.concatenate(
            [got[q, DIRECT : 2 * DIRECT, :], spill[place, SPILL : 2 * SPILL, :]], axis=0
        )
        both = jnp.concatenate([rows_phi, rows_stress], axis=1)
        both = jnp.dot(pick, both, precision=exact, preferred_element_type=jnp.float32)
        phi = both[:, :SITES]
        stress = both[:, SITES:]
        s0 = micro[base : base + cap, :]
        s1 = s0 / (1.0 + 0.2 * phi * s0)
        micro_out[base : base + cap, :] = s1
        flow = 0.1 * phi * s1 * stress
        parts = []
        for l0 in range(0, cap, 8):
            l1 = min(l0 + 8, cap)
            old = chain[base + l0 : base + l1]
            decay = jnp.exp(phi[l0:l1][:, None, :] * speed[None])
            new = decay * old + 0.15 * (1.0 - decay) * stress[l0:l1][:, None, :]
            chain_out[base + l0 : base + l1] = new
            kelvin = jnp.sum(new - old, axis=1)
            parts.append(solid[l0:l1] * kelvin + flow[l0:l1])
        slots = jnp.concatenate(parts, axis=0)
        result = lax.dot_general(
            pick, slots, (((0,), (0,)), ((), ())),
            precision=exact, preferred_element_type=jnp.float32,
        )
        change[q] = result[:DIRECT]
        change_spill[place] = result[DIRECT:]


def send_back_lean(
    n_gz, n_gy, change, spill, where, out,
    back, tmp, half, pair, line, ends, out_sems, in_sems, relay_out, relay_in,
):
    n = n_gz * n_gy
    rows, cols = out.shape
    depth = n // 8
    gz = lax.axis_index("gz")
    gy = lax.axis_index("gy")
    me = gz * n_gy + gy
    z, x = gz // 2, lax.rem(gz, 2)
    y, core = gy // 2, lax.rem(gy, 2)
    greet_all(n, n_gy, me)

    def relay(src, dst, sem, arrived, to):
        return pltpu.make_async_remote_copy(
            src_ref=src, dst_ref=dst,
            send_sem=relay_out.at[sem], recv_sem=relay_in.at[arrived],
            device_id=to, device_id_type=MESH,
        )

    across = relay(
        spill.at[pl.ds((1 - core) * 4 * depth, 4 * depth)],
        tmp.at[pl.ds(0, 4 * depth)], depth + 2, depth + 2, (gz, y * 2 + 1 - core),
    )
    across.start()

    def row_copy(o, at):
        return pltpu.make_async_remote_copy(
            src_ref=change.at[o],
            dst_ref=back.at[pl.ds(pl.multiple_of(at * DIRECT, 8), DIRECT)],
            send_sem=out_sems.at[o],
            recv_sem=in_sems.at[at],
            device_id=(o // n_gy, lax.rem(o, n_gy)),
            device_id_type=MESH,
        )

    def push(i, carry):
        row_copy(partner(i, n, me), me).start()
        return carry

    lax.fori_loop(0, n - 1, push, 0)
    back[pl.ds(pl.multiple_of(me * DIRECT, 8), DIRECT), :] = change[me]

    across.wait_recv()
    half[...] = spill[pl.ds(core * 4 * depth, 4 * depth)] + tmp[0 : 4 * depth]
    along = relay(
        half.at[pl.ds((1 - x) * 2 * depth, 2 * depth)],
        tmp.at[pl.ds(4 * depth, 2 * depth)], depth + 1, depth + 1, (z * 2 + 1 - x, gy),
    )
    along.start()
    along.wait_recv()
    pair[...] = half[pl.ds(x * 2 * depth, 2 * depth)] + tmp[4 * depth : 6 * depth]
    beside = relay(
        pair.at[pl.ds((1 - y) * depth, depth)],
        tmp.at[pl.ds(6 * depth, depth)], depth, depth, (gz, (1 - y) * 2 + core),
    )
    beside.start()
    beside.wait_recv()
    line[...] = pair[pl.ds(y * depth, depth)] + tmp[6 * depth : 7 * depth]

    def end_copy(d):
        to = lax.rem(z + d, depth)
        return relay(line.at[to], ends.at[depth - d], d, depth - d, (to * 2 + x, gy))

    for d in range(1, depth):
        end_copy(d).start()
    total = line[z]
    for d in range(1, depth):
        end_copy(d).wait_recv()
    for d in range(1, depth):
        total = total + ends[d]
    back[n * DIRECT : n * DIRECT + SPILL, :] = total

    across.wait_send()
    along.wait_send()
    beside.wait_send()
    for d in range(1, depth):
        end_copy(d).wait_send()

    def finish(i, carry):
        o = partner(i, n, me)
        row_copy(o, o).wait()
        return carry

    lax.fori_loop(0, n - 1, finish, 0)
    per_row = cols // SITES

    def place(g, carry):
        r = pl.multiple_of(g * 8, 8)
        for j in range(per_row):
            lines = [back[pl.ds(where[(r + k) * per_row + j], 1), :] for k in range(8)]
            out[pl.ds(r, 8), j * SITES : (j + 1) * SITES] = jnp.concatenate(lines, axis=0)
        return carry

    lax.fori_loop(0, rows // 8, place, 0)


def send_back(n_gz, n_gy, change, where, out, back, out_sems, in_sems):
    n = n_gz * n_gy
    rows, cols = out.shape
    cp = change.shape[1]
    me = lax.axis_index("gz") * n_gy + lax.axis_index("gy")
    greet_all(n, n_gy, me)

    def push(i, carry):
        o = partner(i, n, me)
        pltpu.make_async_remote_copy(
            src_ref=change.at[o],
            dst_ref=back.at[pl.ds(pl.multiple_of(me * cp, 8), cp)],
            send_sem=out_sems.at[o],
            recv_sem=in_sems.at[me],
            device_id=(o // n_gy, lax.rem(o, n_gy)),
            device_id_type=MESH,
        ).start()
        return carry

    lax.fori_loop(0, n - 1, push, 0)
    back[pl.ds(pl.multiple_of(me * cp, 8), cp), :] = change[me]

    def finish(i, carry):
        o = partner(i, n, me)
        pltpu.make_async_remote_copy(
            src_ref=change.at[o],
            dst_ref=back.at[pl.ds(pl.multiple_of(o * cp, 8), cp)],
            send_sem=out_sems.at[o],
            recv_sem=in_sems.at[o],
            device_id=(o // n_gy, lax.rem(o, n_gy)),
            device_id_type=MESH,
        ).wait()
        return carry

    lax.fori_loop(0, n - 1, finish, 0)
    per_row = cols // SITES

    def place(g, carry):
        r = pl.multiple_of(g * 8, 8)
        for j in range(per_row):
            lines = [back[pl.ds(where[(r + k) * per_row + j], 1), :] for k in range(8)]
            out[pl.ds(r, 8), j * SITES : (j + 1) * SITES] = jnp.concatenate(lines, axis=0)
        return carry

    lax.fori_loop(0, rows // 8, place, 0)


def body(n_gz, n_gy, warmth, moisture, degree, tally, keeper, pouring, chain, micro):
    n = n_gz * n_gy
    rows, cols = warmth.shape
    per_row = cols // SITES
    slots = chain.shape[0]
    cap = slots // n
    cp = padded_rows(cap + 1)
    nb = rows * per_row
    lifts = rows // LIFT
    vm = pl.BlockSpec(memory_space=pltpu.VMEM)
    sm = pl.BlockSpec(memory_space=pltpu.SMEM)
    hbm = pl.BlockSpec(memory_space=pl.ANY)
    f32 = jnp.float32

    local_times = lax.dynamic_slice_in_dim(pouring, lax.axis_index("gz") * lifts, lifts)
    age = 2400.0 - jnp.repeat(local_times, LIFT).astype(f32)
    solid = jnp.sqrt(600.0 / age) + 0.2
    flat = keeper.reshape(-1)
    slot_id = jnp.arange(slots, dtype=jnp.int32)
    hit = flat[None, :] == slot_id[:, None]
    block = jnp.arange(nb, dtype=jnp.int32)
    held = (block % per_row) * rows + block // per_row
    solid_slot = jnp.sum(jnp.where(hit, jnp.repeat(solid, per_row)[None, :], 0.0), axis=1)
    solid_rows = jnp.pad(solid_slot.reshape(n, cap), ((0, 0), (0, SITES - cap)))
    lean = cap >= DIRECT + 8 and n % 8 == 0 and n_gy == 4
    owner = flat // cap
    earlier = flat[None, :] < flat[:, None]
    if lean:
        rank = jnp.sum(earlier & (owner[None, :] == owner[:, None]), axis=1, dtype=jnp.int32)
        over = rank >= DIRECT
        spot = jnp.sum(earlier & over[None, :], axis=1, dtype=jnp.int32)
        spilled = jnp.sum(over, dtype=jnp.int32)
        code = jnp.where(over, DIRECT + spot, rank)
        slot_map = jnp.sum(jnp.where(hit, code[None, :] + 1, 0), axis=1) - 1
        target = jnp.where(over, n * DIRECT + spot, owner * DIRECT + rank)
        line_id = jnp.arange(n * DIRECT + SPILL, dtype=jnp.int32)
        fits = target[None, :] == line_id[:, None]
        index = nb + jnp.sum(jnp.where(fits, held[None, :] - nb, 0), axis=1)
        index, spill_index = index[: n * DIRECT], index[n * DIRECT :]
        slot_map = jnp.pad(slot_map.reshape(n, cap).astype(f32), ((0, 0), (0, SITES - cap)))
        count = jnp.broadcast_to(spilled.astype(f32), (n, SITES))
        where_back = jnp.minimum(target, n * DIRECT + SPILL - 1)
        notes = [slot_map, solid_rows, count]
    else:
        index = spill_index = jnp.zeros((8,), jnp.int32)
        notes = [solid_rows, solid_rows, solid_rows]
    notes = jnp.stack(notes + [jnp.zeros((n, SITES), f32)] * 5, axis=1)

    field = jax.ShapeDtypeStruct((rows, cols), f32)
    outs = [field, field, field, jax.ShapeDtypeStruct((2, nb + 8, SITES), f32)]
    outs += [jax.ShapeDtypeStruct((n, 8, SITES), f32)]
    scratch = [
        pltpu.VMEM((SWEEPS, 2, rows + 2 * TOP, cols + 2 * PAD), f32),
        pltpu.VMEM((rows + 2 * TOP, cols + 2 * PAD), f32),
        pltpu.VMEM((SWEEPS, 2, 2, cols), f32),
        pltpu.VMEM((SWEEPS, 2, 2, cols), f32),
        pltpu.SemaphoreType.DMA((SWEEPS, 2, 2)),
        pltpu.SemaphoreType.DMA((SWEEPS, 2, 2)),
        pltpu.SemaphoreType.DMA((n,)),
        pltpu.SemaphoreType.DMA((n,)),
    ]
    out_specs = [vm] * 5
    if lean:
        outs += [jax.ShapeDtypeStruct((n, 2 * DIRECT, SITES), f32)]
        outs += [jax.ShapeDtypeStruct((n, 2 * SPILL, SITES), f32)]
        out_specs += [hbm, vm]
        scratch += [
            pltpu.VMEM((n, 2 * DIRECT, SITES), f32),
            pltpu.SemaphoreType.DMA((n,)),
            pltpu.SemaphoreType.DMA((n,)),
            pltpu.SemaphoreType.DMA,
            pltpu.SemaphoreType.DMA((n // 8 + 3,)),
            pltpu.SemaphoreType.DMA((n // 8 + 3,)),
        ]
    limit = 40 * 1024 * 1024
    results = pl.pallas_call(
        functools.partial(sweep_and_send, n_gz, n_gy, lean),
        out_shape=tuple(outs),
        in_specs=[vm, vm, vm, vm, sm, sm, vm],
        out_specs=tuple(out_specs),
        scratch_shapes=scratch,
        compiler_params=pltpu.CompilerParams(
            collective_id=0, has_side_effects=True, vmem_limit_bytes=limit
        ),
        name="sweep_and_send",
    )(warmth, moisture, degree, tally, index, spill_index, notes)
    temp, hum, degree_after, blocks, notes_in = results[:5]

    state_specs = (
        pl.BlockSpec((GROUP * cap, KU, SITES), lambda i: (i, 0, 0)),
        pl.BlockSpec((GROUP * cap, SITES), lambda i: (i, 0)),
    )
    state_shapes = (
        jax.ShapeDtypeStruct(chain.shape, f32),
        jax.ShapeDtypeStruct(micro.shape, f32),
    )

    def dense_tail(*_):
        index = nb + jnp.sum(jnp.where(hit, held[None, :] - nb, 0), axis=1)
        where = (flat // cap) * cp + flat % cap
        got = pl.pallas_call(
            functools.partial(send_dense, n_gz, n_gy, cap),
            out_shape=jax.ShapeDtypeStruct((n, 2 * cp, SITES), f32),
            in_specs=[vm, sm, vm],
            out_specs=hbm,
            scratch_shapes=[
                pltpu.VMEM((n, 2 * cp, SITES), f32),
                pltpu.SemaphoreType.DMA((n,)),
                pltpu.SemaphoreType.DMA((n,)),
                pltpu.SemaphoreType.DMA,
            ],
            compiler_params=pltpu.CompilerParams(
                collective_id=2, has_side_effects=True, vmem_limit_bytes=limit
            ),
            name="send_dense",
        )(blocks, index, solid_rows)
        chain_after, micro_after, change = pl.pallas_call(
            functools.partial(creep, cap),
            grid=(n // GROUP,),
            out_shape=state_shapes + (jax.ShapeDtypeStruct((n, cp, SITES), f32),),
            in_specs=[pl.BlockSpec((GROUP, 2 * cp, SITES), lambda i: (i, 0, 0)), *state_specs],
            out_specs=(*state_specs, pl.BlockSpec((GROUP, cp, SITES), lambda i: (i, 0, 0))),
            compiler_params=pltpu.CompilerParams(vmem_limit_bytes=limit),
            name="creep",
        )(got, chain, micro)
        cells = pl.pallas_call(
            functools.partial(send_back, n_gz, n_gy),
            out_shape=field,
            in_specs=[vm, sm],
            out_specs=vm,
            scratch_shapes=[
                pltpu.VMEM((n * cp, SITES), f32),
                pltpu.SemaphoreType.DMA((n,)),
                pltpu.SemaphoreType.DMA((n,)),
            ],
            compiler_params=pltpu.CompilerParams(
                collective_id=1, has_side_effects=True, vmem_limit_bytes=limit
            ),
            name="send_back",
        )(change, where)
        return cells, chain_after, micro_after

    def lean_tail(got, got_spill):
        depth = n // 8
        whole = pl.BlockSpec((n, SPILL, SITES), lambda i: (0, 0, 0))
        chain_after, micro_after, change, change_spill = pl.pallas_call(
            functools.partial(creep_lean, cap, depth),
            grid=(n // GROUP,),
            out_shape=state_shapes
            + (
                jax.ShapeDtypeStruct((n, DIRECT, SITES), f32),
                jax.ShapeDtypeStruct((n, SPILL, SITES), f32),
            ),
            in_specs=[
                pl.BlockSpec((GROUP, 2 * DIRECT, SITES), lambda i: (i, 0, 0)),
                pl.BlockSpec((n, 2 * SPILL, SITES), lambda i: (0, 0, 0)),
                pl.BlockSpec((GROUP, 8, SITES), lambda i: (i, 0, 0)),
                *state_specs,
            ],
            out_specs=(
                *state_specs,
                pl.BlockSpec((GROUP, DIRECT, SITES), lambda i: (i, 0, 0)),
                whole,
            ),
            compiler_params=pltpu.CompilerParams(vmem_limit_bytes=limit),
            name="creep_lean",
        )(got, got_spill, notes_in, chain, micro)
        cells = pl.pallas_call(
            functools.partial(send_back_lean, n_gz, n_gy),
            out_shape=field,
            in_specs=[vm, vm, sm],
            out_specs=vm,
            scratch_shapes=[
                pltpu.VMEM((n * DIRECT + SPILL, SITES), f32),
                pltpu.VMEM((7 * depth, SPILL, SITES), f32),
                pltpu.VMEM((4 * depth, SPILL, SITES), f32),
                pltpu.VMEM((2 * depth, SPILL, SITES), f32),
                pltpu.VMEM((depth, SPILL, SITES), f32),
                pltpu.VMEM((depth, SPILL, SITES), f32),
                pltpu.SemaphoreType.DMA((n,)),
                pltpu.SemaphoreType.DMA((n,)),
                pltpu.SemaphoreType.DMA((depth + 3,)),
                pltpu.SemaphoreType.DMA((depth + 3,)),
            ],
            compiler_params=pltpu.CompilerParams(
                collective_id=3, has_side_effects=True, vmem_limit_bytes=limit
            ),
            name="send_back_lean",
        )(change, change_spill, where_back)
        return cells, chain_after, micro_after

    if lean:
        fits_all = jnp.max(notes_in[:, 2, 0]) <= SPILL
        creep_cells, chain_after, micro_after = lax.cond(
            fits_all, lean_tail, dense_tail, *results[5:]
        )
    else:
        creep_cells, chain_after, micro_after = dense_tail()
    return temp, hum, degree_after, creep_cells, chain_after, micro_after


def solution(mesh):
    n_gz, n_gy = mesh.shape["gz"], mesh.shape["gy"]
    cells = P("gz", "gy")
    states = P(("gz", "gy"), None, None)
    tension = P(("gz", "gy"), None)
    return jax.shard_map(
        functools.partial(body, n_gz, n_gy),
        mesh=mesh,
        in_specs=(cells, cells, cells, cells, cells, P(), states, tension),
        out_specs=(cells, cells, cells, cells, states, tension),
        check_vma=False,
    )
```

```python
import functools

import jax
import jax.numpy as jnp
from jax import lax
from jax.experimental import pallas as pl
from jax.experimental.pallas import tpu as pltpu
from jax.sharding import PartitionSpec as P

NX = 48
SITES = 128
KU = 8
SWEEPS = 3
LIFT = 8
PAD = 128
TOP = 8
GROUP = 4
DIRECT = 24
SPILL = 40
DRY = 0.05 + 0.95 / (1.0 + 5.0**16)
MESH = pl.DeviceIdType.MESH


def rate(temp, hum, degree):
    term = 7.5 - 7.5 * hum
    term = term * term
    return 0.05 * (1.0 - degree) * jnp.exp(0.5 * temp) / (1.0 + term * term)


def diffusivity(hum):
    ratio = 5.0 * (1.0 - hum)
    power = ratio * ratio
    power = power * power
    power = power * power
    power = power * power
    return 0.05 + 0.95 / (1.0 + power)


def padded_rows(count):
    return -(-count // 8) * 8


def greet_all(n, n_gy, me):
    barrier = pltpu.get_barrier_semaphore()

    def greet(j, carry):
        other = lax.rem(me + 1 + j, n)
        pl.semaphore_signal(
            barrier, inc=1, device_id=(other // n_gy, lax.rem(other, n_gy)), device_id_type=MESH
        )
        return carry

    lax.fori_loop(0, n - 1, greet, 0)
    pl.semaphore_wait(barrier, n - 1)


def partner(i, n, me):
    return lax.rem(me + 1 + lax.rem(i + n // 2 - 1, n - 1), n)


def sweep_and_send(
    n_gz, n_gy, lean,
    warmth, moisture, degree, tally, index, spill_index, notes,
    temp_out, hum_out, degree_out, blocks, notes_in, *rest,
):
    if lean:
        got, got_spill = rest[:2]
        rest = rest[2:]
    ext, diff, z_send, z_recv, z_sems, y_sems, note_out, note_in = rest[:8]
    if lean:
        send, out_sems, in_sems, own_sems, relay_out, relay_in = rest[8:]
    n = n_gz * n_gy
    rows, cols = warmth.shape
    wide = cols + 2 * PAD
    per_row = cols // SITES
    gz = lax.axis_index("gz")
    gy = lax.axis_index("gy")
    me = gz * n_gy + gy
    greet_all(n, n_gy, me)

    def note_copy(o, at):
        return pltpu.make_async_remote_copy(
            src_ref=notes.at[o],
            dst_ref=notes_in.at[at],
            send_sem=note_out.at[o],
            recv_sem=note_in.at[at],
            device_id=(o // n_gy, lax.rem(o, n_gy)),
            device_id_type=MESH,
        )

    def tell(i, carry):
        note_copy(partner(i, n, me), me).start()
        return carry

    x = lax.rem(lax.broadcasted_iota(jnp.int32, (8, cols), 1), NX)
    has_west = x > 0
    has_east = x < NX - 1
    inner = slice(PAD, PAD + cols)
    body_rows = slice(TOP, TOP + rows)

    ext[0, 0, body_rows, inner] = warmth[...]
    ext[0, 1, body_rows, inner] = moisture[...]

    for s in range(SWEEPS):
        for f in range(2):
            z_send[s, 0, f : f + 1] = ext[s, f, TOP : TOP + 1, inner]
            z_send[s, 1, f : f + 1] = ext[s, f, TOP + rows - 1 : TOP + rows, inner]

        def z_copy(side, s=s):
            to = gz - 1 + 2 * side
            return pltpu.make_async_remote_copy(
                src_ref=z_send.at[s, side],
                dst_ref=z_recv.at[s, 1 - side],
                send_sem=z_sems.at[s, 0, side],
                recv_sem=z_sems.at[s, 1, 1 - side],
                device_id=(to, gy),
                device_id_type=MESH,
            )

        def y_copy(side, s=s):
            to = gy - 1 + 2 * side
            a = PAD if side == 0 else cols
            b = PAD + cols if side == 0 else 0
            return pltpu.make_async_remote_copy(
                src_ref=ext.at[s, :, body_rows, pl.ds(a, PAD)],
                dst_ref=ext.at[s, :, body_rows, pl.ds(b, PAD)],
                send_sem=y_sems.at[s, 0, side],
                recv_sem=y_sems.at[s, 1, 1 - side],
                device_id=(gz, to),
                device_id_type=MESH,
            )

        there = (gz > 0, gz < n_gz - 1)
        beside = (gy > 0, gy < n_gy - 1)
        for side in range(2):
            pl.when(beside[side])(lambda side=side: y_copy(side).start())
            pl.when(there[side])(lambda side=side: z_copy(side).start())

        if s == 0:
            lax.fori_loop(0, n - 1, tell, 0)
            notes_in[me] = notes[me]

        for side in range(2):

            @pl.when(jnp.logical_not(there[side]))
            def _(side=side, s=s):
                z_recv[s, side] = jnp.zeros((2, cols), jnp.float32)

            @pl.when(jnp.logical_not(beside[side]))
            def _(side=side, s=s):
                b = 0 if side == 0 else PAD + cols
                ext[s, :, body_rows, pl.ds(b, PAD)] = jnp.zeros((2, rows, PAD), jnp.float32)

        for side in range(2):
            pl.when(there[side])(lambda side=side: z_copy(1 - side).wait_recv())
            pl.when(beside[side])(lambda side=side: y_copy(1 - side).wait_recv())

        for f in range(2):
            ext[s, f, TOP - 1 : TOP, inner] = z_recv[s, 0, f : f + 1]
            ext[s, f, TOP + rows : TOP + rows + 1, inner] = z_recv[s, 1, f : f + 1]
        diff[TOP - 1 : TOP, inner] = diffusivity(z_recv[s, 0, 1:2])
        diff[TOP + rows : TOP + rows + 1, inner] = diffusivity(z_recv[s, 1, 1:2])
        for r in range(0, rows, 8):
            here = slice(TOP + r, TOP + r + 8)
            diff[here, :] = diffusivity(ext[s, 1, here, :])

        for r in range(0, rows, 8):
            here = slice(TOP + r, TOP + r + 8)
            up = slice(TOP + r + 1, TOP + r + 9)
            down = slice(TOP + r - 1, TOP + r + 7)
            own = slice(r, r + 8)
            temp = ext[s, 0, here, :]
            hum = ext[s, 1, here, :]
            cond = diff[here, :]

            def aside(v, shift):
                return pltpu.roll(v, shift % wide, 1)[:, inner]

            total = (
                ext[s, 0, up, inner] + ext[s, 0, down, inner] + aside(temp, -NX) + aside(temp, NX)
            )
            total = total + jnp.where(has_east, aside(temp, -1), 0.0)
            total = total + jnp.where(has_west, aside(temp, 1), 0.0)
            t0 = temp[:, inner]
            h0 = hum[:, inner]
            d0 = cond[:, inner]
            progress = rate(t0, h0, degree[own, :])
            near = [
                (ext[s, 1, up, inner], diff[up, inner]),
                (ext[s, 1, down, inner], diff[down, inner]),
                (aside(hum, -NX), aside(cond, -NX)),
                (aside(hum, NX), aside(cond, NX)),
                (
                    jnp.where(has_east, aside(hum, -1), 0.0),
                    jnp.where(has_east, aside(cond, -1), DRY),
                ),
                (
                    jnp.where(has_west, aside(hum, 1), 0.0),
                    jnp.where(has_west, aside(cond, 1), DRY),
                ),
            ]
            conduct = None
            inflow = None
            for g, dg in near:
                c = 0.5 * (d0 + dg)
                conduct = c if conduct is None else conduct + c
                inflow = c * g if inflow is None else inflow + c * g
            t1 = (warmth[own, :] + 4.0 * progress + total) / 7.0
            h1 = (moisture[own, :] - 0.5 * progress + inflow) / (1.0 + conduct)
            if s < SWEEPS - 1:
                ext[s + 1, 0, here, inner] = t1
                ext[s + 1, 1, here, inner] = h1
            else:
                temp_out[own, :] = t1
                hum_out[own, :] = h1
                a1 = degree[own, :] + rate(t1, h1, degree[own, :])
                degree_out[own, :] = a1
                stress = -a1 * (0.5 * t1 + 2.0 * (1.0 - h1))
                phi = jnp.exp(0.3 * t1) * (0.1 + 0.9 * h1 * h1)
                lane = lax.broadcasted_iota(jnp.int32, (8, SITES), 1)
                for j in range(per_row):
                    cut = slice(j * SITES, (j + 1) * SITES)
                    at = slice(j * rows + r, j * rows + r + 8)
                    placed = lane < tally[own, j : j + 1]
                    blocks[0, at, :] = jnp.where(placed, phi[:, cut], 0.0)
                    blocks[1, at, :] = jnp.where(placed, stress[:, cut], 0.0)

    nb = rows * per_row
    blocks[0, nb : nb + 8, :] = jnp.zeros((8, SITES), jnp.float32)
    blocks[1, nb : nb + 8, :] = jnp.zeros((8, SITES), jnp.float32)

    if lean:
        z, x = gz // 2, lax.rem(gz, 2)
        y, core = gy // 2, lax.rem(gy, 2)
        depth = n // 8

        def spill_copy(sem, arrived, base, count, to):
            part = got_spill.at[pl.ds(base, count)]
            return pltpu.make_async_remote_copy(
                src_ref=part,
                dst_ref=part,
                send_sem=relay_out.at[sem],
                recv_sem=relay_in.at[arrived],
                device_id=to,
                device_id_type=MESH,
            )

        line = (core * 4 + x * 2 + y) * depth
        for l in range(SPILL):
            k = spill_index[l]
            got_spill[line + z, l : l + 1, :] = blocks[0, pl.ds(k, 1), :]
            got_spill[line + z, SPILL + l : SPILL + l + 1, :] = blocks[1, pl.ds(k, 1), :]

        def z_other(d):
            return lax.rem(z + d, depth)

        for d in range(1, depth):
            spill_copy(d, depth - d, line + z, 1, (z_other(d) * 2 + x, gy)).start()

        def fill(o):
            for l in range(DIRECT):
                k = index[o * DIRECT + l]
                send[o, l : l + 1, :] = blocks[0, pl.ds(k, 1), :]
                send[o, DIRECT + l : DIRECT + l + 1, :] = blocks[1, pl.ds(k, 1), :]

        def row_copy(o, at):
            return pltpu.make_async_remote_copy(
                src_ref=send.at[o],
                dst_ref=got.at[at],
                send_sem=out_sems.at[o],
                recv_sem=in_sems.at[at],
                device_id=(o // n_gy, lax.rem(o, n_gy)),
                device_id_type=MESH,
            )

        def push(i, carry):
            o = partner(i, n, me)
            fill(o)
            row_copy(o, me).start()
            return carry

        lax.fori_loop(0, n - 1, push, 0)
        fill(me)
        own_copy = pltpu.make_async_copy(send.at[me], got.at[me], own_sems)
        own_copy.start()

        for d in range(1, depth):
            spill_copy(d, depth - d, line + z_other(d), 1, (z_other(d) * 2 + x, gy)).wait_recv()
        spill_copy(depth, depth, line, depth, (gz, (1 - y) * 2 + core)).start()
        other = (core * 4 + x * 2 + 1 - y) * depth
        spill_copy(depth, depth, other, depth, (gz, (1 - y) * 2 + core)).wait_recv()
        pair = (core * 4 + x * 2) * depth
        spill_copy(depth + 1, depth + 1, pair, 2 * depth, (z * 2 + 1 - x, gy)).start()
        other = (core * 4 + (1 - x) * 2) * depth
        spill_copy(depth + 1, depth + 1, other, 2 * depth, (z * 2 + 1 - x, gy)).wait_recv()
        half = core * 4 * depth
        spill_copy(depth + 2, depth + 2, half, 4 * depth, (gz, y * 2 + 1 - core)).start()
        other = (1 - core) * 4 * depth
        spill_copy(depth + 2, depth + 2, other, 4 * depth, (gz, y * 2 + 1 - core)).wait_recv()

        for d in range(1, depth):
            spill_copy(d, depth - d, line + z, 1, (z_other(d) * 2 + x, gy)).wait_send()
        spill_copy(depth, depth, line, depth, (gz, (1 - y) * 2 + core)).wait_send()
        spill_copy(depth + 1, depth + 1, pair, 2 * depth, (z * 2 + 1 - x, gy)).wait_send()
        spill_copy(depth + 2, depth + 2, half, 4 * depth, (gz, y * 2 + 1 - core)).wait_send()

    for s in range(SWEEPS):
        for side in range(2):
            a = PAD if side == 0 else cols
            pl.when((gz > 0, gz < n_gz - 1)[side])(
                lambda s=s, side=side: pltpu.make_async_remote_copy(
                    src_ref=z_send.at[s, side],
                    dst_ref=z_recv.at[s, 1 - side],
                    send_sem=z_sems.at[s, 0, side],
                    recv_sem=z_sems.at[s, 1, 1 - side],
                    device_id=(gz - 1 + 2 * side, gy),
                    device_id_type=MESH,
                ).wait_send()
            )
            pl.when((gy > 0, gy < n_gy - 1)[side])(
                lambda s=s, side=side, a=a: pltpu.make_async_remote_copy(
                    src_ref=ext.at[s, :, body_rows, pl.ds(a, PAD)],
                    dst_ref=ext.at[s, :, body_rows, pl.ds(a, PAD)],
                    send_sem=y_sems.at[s, 0, side],
                    recv_sem=y_sems.at[s, 1, 1 - side],
                    device_id=(gz, gy - 1 + 2 * side),
                    device_id_type=MESH,
                ).wait_send()
            )

    def told(i, carry):
        o = partner(i, n, me)
        note_copy(o, o).wait()
        return carry

    lax.fori_loop(0, n - 1, told, 0)

    if lean:
        own_copy.wait()

        def finish(i, carry):
            o = partner(i, n, me)
            row_copy(o, o).wait()
            return carry

        lax.fori_loop(0, n - 1, finish, 0)


def send_dense(
    n_gz, n_gy, cap, blocks, index, solid, got, send, out_sems, in_sems, own_sem
):
    n = n_gz * n_gy
    cp = padded_rows(cap + 1)
    me = lax.axis_index("gz") * n_gy + lax.axis_index("gy")
    greet_all(n, n_gy, me)

    def row_copy(o, at):
        return pltpu.make_async_remote_copy(
            src_ref=send.at[o],
            dst_ref=got.at[at],
            send_sem=out_sems.at[o],
            recv_sem=in_sems.at[at],
            device_id=(o // n_gy, lax.rem(o, n_gy)),
            device_id_type=MESH,
        )

    def fill(o):
        for l in range(cap):
            k = index[o * cap + l]
            send[o, l : l + 1, :] = blocks[0, pl.ds(k, 1), :]
            send[o, cp + l : cp + l + 1, :] = blocks[1, pl.ds(k, 1), :]
        send[o, cap : cap + 1, :] = solid[pl.ds(o, 1), :]

    def push(i, carry):
        o = partner(i, n, me)
        fill(o)
        row_copy(o, me).start()
        return carry

    lax.fori_loop(0, n - 1, push, 0)
    fill(me)
    own_copy = pltpu.make_async_copy(send.at[me], got.at[me], own_sem)
    own_copy.start()
    own_copy.wait()

    def finish(i, carry):
        o = partner(i, n, me)
        row_copy(o, o).wait()
        return carry

    lax.fori_loop(0, n - 1, finish, 0)


def creep(cap, got, chain, micro, chain_out, micro_out, change):
    cp = padded_rows(cap + 1)
    unit = lax.broadcasted_iota(jnp.int32, (KU, SITES), 0)
    speed = jnp.full((KU, SITES), -10.0, jnp.float32)
    for m in range(1, KU):
        speed = jnp.where(unit == m, -10.0 / 3.0**m, speed)
    sub = lax.broadcasted_iota(jnp.int32, (cap, SITES), 0)
    lane = lax.broadcasted_iota(jnp.int32, (cap, SITES), 1)
    for q in range(GROUP):
        base = q * cap
        phi = got[q, 0:cap, :]
        stress = got[q, cp : cp + cap, :]
        row = got[q, cap : cap + 1, :]
        solid = jnp.sum(jnp.where(sub == lane, row, 0.0), axis=1, keepdims=True)
        s0 = micro[base : base + cap, :]
        s1 = s0 / (1.0 + 0.2 * phi * s0)
        micro_out[base : base + cap, :] = s1
        flow = 0.1 * phi * s1 * stress
        for l0 in range(0, cap, 8):
            l1 = min(l0 + 8, cap)
            old = chain[base + l0 : base + l1]
            decay = jnp.exp(phi[l0:l1][:, None, :] * speed[None])
            new = decay * old + 0.15 * (1.0 - decay) * stress[l0:l1][:, None, :]
            chain_out[base + l0 : base + l1] = new
            kelvin = jnp.sum(new - old, axis=1)
            change[q, l0:l1, :] = solid[l0:l1] * kelvin + flow[l0:l1]
        change[q, cap:cp, :] = jnp.zeros((cp - cap, SITES), jnp.float32)


def creep_and_return(
    n_gz, n_gy, cap,
    got, spill, notes, micro, where, chain,
    out, micro_out, chain_out,
    old_state, new_state, change, back, read_sems, write_sems, out_sems, in_sems,
):
    n = n_gz * n_gy
    depth = n // 8
    rows, cols = out.shape
    gz = lax.axis_index("gz")
    gy = lax.axis_index("gy")
    me = gz * n_gy + gy
    held = DIRECT + SPILL
    part = n_gy * cap

    def read(g):
        at = pl.ds(g * part, part)
        return pltpu.make_async_copy(chain.at[at], old_state.at[at], read_sems.at[g])

    def write(g):
        at = pl.ds(g * part, part)
        return pltpu.make_async_copy(new_state.at[at], chain_out.at[at], write_sems.at[g])

    def turn(i):
        return lax.rem(gz + n_gz // 2 + i, n_gz)

    def begin(i, carry):
        read(turn(i)).start()
        return carry

    lax.fori_loop(0, n_gz, begin, 0)
    greet_all(n, n_gy, me)

    unit = lax.broadcasted_iota(jnp.int32, (KU, SITES), 0)
    speed = jnp.full((KU, SITES), -10.0, jnp.float32)
    for m in range(1, KU):
        speed = jnp.where(unit == m, -10.0 / 3.0**m, speed)
    tall = -(-cap // 16) * 16
    sub = lax.broadcasted_iota(jnp.int32, (tall, SITES), 0)
    lane = lax.broadcasted_iota(jnp.int32, (tall, SITES), 1)
    row_id = lax.rem(lax.broadcasted_iota(jnp.int32, (tall, 3 * held), 1), held)
    row_id = row_id.astype(jnp.float32)

    def row_copy(o, at):
        return pltpu.make_async_remote_copy(
            src_ref=change.at[o],
            dst_ref=back.at[at],
            send_sem=out_sems.at[o],
            recv_sem=in_sems.at[at],
            device_id=(o // n_gy, lax.rem(o, n_gy)),
            device_id_type=MESH,
        )

    def group(i, carry):
        g = turn(i)
        read(g).wait()
        start = pl.multiple_of(g * part, 8)
        s0 = micro[pl.ds(start, part), :]
        z, x = g // 2, lax.rem(g, 2)
        all_phi = []
        all_stress = []
        all_solid = []
        for q in range(n_gy):
            o = g * n_gy + q
            place = (q % 2 * 4 + x * 2 + q // 2) * depth + z

            def column(r):
                row = notes[o, r : r + 1, :]
                return jnp.sum(jnp.where(sub == lane, row, 0.0), axis=1, keepdims=True)

            pick = jnp.where(column(0) == row_id, 1.0, 0.0).astype(jnp.bfloat16)
            all_solid.append(column(1)[:cap])
            rows_phi = jnp.concatenate([got[o, 0:DIRECT, :], spill[place, 0:SPILL, :]], axis=0)
            rows_stress = jnp.concatenate(
                [got[o, DIRECT : 2 * DIRECT, :], spill[place, SPILL : 2 * SPILL, :]], axis=0
            )
            both = jnp.concatenate([rows_phi, rows_stress], axis=1)
            high = both.astype(jnp.bfloat16)
            left = both - high.astype(jnp.float32)
            middle = left.astype(jnp.bfloat16)
            low = (left - middle.astype(jnp.float32)).astype(jnp.bfloat16)
            parts = jnp.concatenate([high, middle, low], axis=0)
            both = jnp.dot(pick, parts, preferred_element_type=jnp.float32)
            all_phi.append(both[:cap, :SITES])
            all_stress.append(both[:cap, SITES:])
        phis = jnp.concatenate(all_phi, axis=0)
        s1 = s0 / (1.0 + 0.2 * phis * s0)
        micro_out[pl.ds(start, part), :] = s1
        for q in range(n_gy):
            o = g * n_gy + q
            phi, stress, solid = all_phi[q], all_stress[q], all_solid[q]
            flow = 0.1 * phi * s1[q * cap : (q + 1) * cap] * stress
            base = g * part + q * cap
            for l0 in range(0, cap, 8):
                l1 = min(l0 + 8, cap)
                at = pl.ds(base + l0, l1 - l0)
                old = old_state[at]
                decay = jnp.exp(phi[l0:l1][:, None, :] * speed[None])
                new = decay * old + 0.15 * (1.0 - decay) * stress[l0:l1][:, None, :]
                new_state[at] = new
                kelvin = jnp.sum(new - old, axis=1)
                change[o, l0:l1, :] = solid[l0:l1] * kelvin + flow[l0:l1]
            pl.when(o != me)(lambda o=o: row_copy(o, me).start())
        write(g).start()
        return carry

    lax.fori_loop(0, n_gz, group, 0)
    back[me] = change[me]

    def finish(i, carry):
        o = partner(i, n, me)
        row_copy(o, o).wait()
        return carry

    lax.fori_loop(0, n - 1, finish, 0)
    per_row = cols // SITES

    def place_cells(g, carry):
        r = pl.multiple_of(g * 8, 8)
        for j in range(per_row):
            lines = []
            for k in range(8):
                w = where[(r + k) * per_row + j]
                lines.append(back[w // 256, pl.ds(lax.rem(w, 256), 1), :])
            out[pl.ds(r, 8), j * SITES : (j + 1) * SITES] = jnp.concatenate(lines, axis=0)
        return carry

    lax.fori_loop(0, rows // 8, place_cells, 0)

    def end(i, carry):
        write(turn(i)).wait()
        return carry

    lax.fori_loop(0, n_gz, end, 0)


def send_back(n_gz, n_gy, change, where, out, back, out_sems, in_sems):
    n = n_gz * n_gy
    rows, cols = out.shape
    cp = change.shape[1]
    me = lax.axis_index("gz") * n_gy + lax.axis_index("gy")
    greet_all(n, n_gy, me)

    def push(i, carry):
        o = partner(i, n, me)
        pltpu.make_async_remote_copy(
            src_ref=change.at[o],
            dst_ref=back.at[pl.ds(pl.multiple_of(me * cp, 8), cp)],
            send_sem=out_sems.at[o],
            recv_sem=in_sems.at[me],
            device_id=(o // n_gy, lax.rem(o, n_gy)),
            device_id_type=MESH,
        ).start()
        return carry

    lax.fori_loop(0, n - 1, push, 0)
    back[pl.ds(pl.multiple_of(me * cp, 8), cp), :] = change[me]

    def finish(i, carry):
        o = partner(i, n, me)
        pltpu.make_async_remote_copy(
            src_ref=change.at[o],
            dst_ref=back.at[pl.ds(pl.multiple_of(o * cp, 8), cp)],
            send_sem=out_sems.at[o],
            recv_sem=in_sems.at[o],
            device_id=(o // n_gy, lax.rem(o, n_gy)),
            device_id_type=MESH,
        ).wait()
        return carry

    lax.fori_loop(0, n - 1, finish, 0)
    per_row = cols // SITES

    def place(g, carry):
        r = pl.multiple_of(g * 8, 8)
        for j in range(per_row):
            lines = [back[pl.ds(where[(r + k) * per_row + j], 1), :] for k in range(8)]
            out[pl.ds(r, 8), j * SITES : (j + 1) * SITES] = jnp.concatenate(lines, axis=0)
        return carry

    lax.fori_loop(0, rows // 8, place, 0)


def body(n_gz, n_gy, warmth, moisture, degree, tally, keeper, pouring, chain, micro):
    n = n_gz * n_gy
    rows, cols = warmth.shape
    per_row = cols // SITES
    slots = chain.shape[0]
    cap = slots // n
    cp = padded_rows(cap + 1)
    nb = rows * per_row
    lifts = rows // LIFT
    vm = pl.BlockSpec(memory_space=pltpu.VMEM)
    sm = pl.BlockSpec(memory_space=pltpu.SMEM)
    hbm = pl.BlockSpec(memory_space=pl.ANY)
    f32 = jnp.float32

    local_times = lax.dynamic_slice_in_dim(pouring, lax.axis_index("gz") * lifts, lifts)
    age = 2400.0 - jnp.repeat(local_times, LIFT).astype(f32)
    solid = jnp.sqrt(600.0 / age) + 0.2
    flat = keeper.reshape(-1)
    slot_id = jnp.arange(slots, dtype=jnp.int32)
    hit = flat[None, :] == slot_id[:, None]
    block = jnp.arange(nb, dtype=jnp.int32)
    held = (block % per_row) * rows + block // per_row
    solid_slot = jnp.sum(jnp.where(hit, jnp.repeat(solid, per_row)[None, :], 0.0), axis=1)
    solid_rows = jnp.pad(solid_slot.reshape(n, cap), ((0, 0), (0, SITES - cap)))
    lean = cap >= DIRECT + 8 and n % 8 == 0 and n_gy == 4 and GROUP * cap % 8 == 0
    owner = flat // cap
    earlier = flat[None, :] < flat[:, None]
    if lean:
        rank = jnp.sum(earlier & (owner[None, :] == owner[:, None]), axis=1, dtype=jnp.int32)
        over = rank >= DIRECT
        spot = jnp.sum(earlier & over[None, :], axis=1, dtype=jnp.int32)
        spilled = jnp.sum(over, dtype=jnp.int32)
        code = jnp.where(over, DIRECT + spot, rank)
        slot_map = jnp.sum(jnp.where(hit, code[None, :] + 1, 0), axis=1) - 1
        target = jnp.where(over, n * DIRECT + spot, owner * DIRECT + rank)
        line_id = jnp.arange(n * DIRECT + SPILL, dtype=jnp.int32)
        fits = target[None, :] == line_id[:, None]
        index = nb + jnp.sum(jnp.where(fits, held[None, :] - nb, 0), axis=1)
        index, spill_index = index[: n * DIRECT], index[n * DIRECT :]
        slot_map = jnp.pad(slot_map.reshape(n, cap).astype(f32), ((0, 0), (0, SITES - cap)))
        count = jnp.broadcast_to(spilled.astype(f32), (n, SITES))
        notes = [slot_map, solid_rows, count]
    else:
        index = spill_index = jnp.zeros((8,), jnp.int32)
        notes = [solid_rows, solid_rows, solid_rows]
    notes = jnp.stack(notes + [jnp.zeros((n, SITES), f32)] * 5, axis=1)

    field = jax.ShapeDtypeStruct((rows, cols), f32)
    outs = [field, field, field, jax.ShapeDtypeStruct((2, nb + 8, SITES), f32)]
    outs += [jax.ShapeDtypeStruct((n, 8, SITES), f32)]
    scratch = [
        pltpu.VMEM((SWEEPS, 2, rows + 2 * TOP, cols + 2 * PAD), f32),
        pltpu.VMEM((rows + 2 * TOP, cols + 2 * PAD), f32),
        pltpu.VMEM((SWEEPS, 2, 2, cols), f32),
        pltpu.VMEM((SWEEPS, 2, 2, cols), f32),
        pltpu.SemaphoreType.DMA((SWEEPS, 2, 2)),
        pltpu.SemaphoreType.DMA((SWEEPS, 2, 2)),
        pltpu.SemaphoreType.DMA((n,)),
        pltpu.SemaphoreType.DMA((n,)),
    ]
    out_specs = [vm] * 5
    if lean:
        outs += [jax.ShapeDtypeStruct((n, 2 * DIRECT, SITES), f32)]
        outs += [jax.ShapeDtypeStruct((n, 2 * SPILL, SITES), f32)]
        out_specs += [hbm, vm]
        scratch += [
            pltpu.VMEM((n, 2 * DIRECT, SITES), f32),
            pltpu.SemaphoreType.DMA((n,)),
            pltpu.SemaphoreType.DMA((n,)),
            pltpu.SemaphoreType.DMA,
            pltpu.SemaphoreType.DMA((n // 8 + 3,)),
            pltpu.SemaphoreType.DMA((n // 8 + 3,)),
        ]
    limit = 40 * 1024 * 1024
    results = pl.pallas_call(
        functools.partial(sweep_and_send, n_gz, n_gy, lean),
        out_shape=tuple(outs),
        in_specs=[vm, vm, vm, vm, sm, sm, vm],
        out_specs=tuple(out_specs),
        scratch_shapes=scratch,
        compiler_params=pltpu.CompilerParams(
            collective_id=0, has_side_effects=True, vmem_limit_bytes=limit
        ),
        name="sweep_and_send",
    )(warmth, moisture, degree, tally, index, spill_index, notes)
    temp, hum, degree_after, blocks, notes_in = results[:5]

    state_specs = (
        pl.BlockSpec((GROUP * cap, KU, SITES), lambda i: (i, 0, 0)),
        pl.BlockSpec((GROUP * cap, SITES), lambda i: (i, 0)),
    )
    state_shapes = (
        jax.ShapeDtypeStruct(chain.shape, f32),
        jax.ShapeDtypeStruct(micro.shape, f32),
    )

    def dense_tail(*_):
        index = nb + jnp.sum(jnp.where(hit, held[None, :] - nb, 0), axis=1)
        where = (flat // cap) * cp + flat % cap
        got = pl.pallas_call(
            functools.partial(send_dense, n_gz, n_gy, cap),
            out_shape=jax.ShapeDtypeStruct((n, 2 * cp, SITES), f32),
            in_specs=[vm, sm, vm],
            out_specs=hbm,
            scratch_shapes=[
                pltpu.VMEM((n, 2 * cp, SITES), f32),
                pltpu.SemaphoreType.DMA((n,)),
                pltpu.SemaphoreType.DMA((n,)),
                pltpu.SemaphoreType.DMA,
            ],
            compiler_params=pltpu.CompilerParams(
                collective_id=2, has_side_effects=True, vmem_limit_bytes=limit
            ),
            name="send_dense",
        )(blocks, index, solid_rows)
        chain_after, micro_after, change = pl.pallas_call(
            functools.partial(creep, cap),
            grid=(n // GROUP,),
            out_shape=state_shapes + (jax.ShapeDtypeStruct((n, cp, SITES), f32),),
            in_specs=[pl.BlockSpec((GROUP, 2 * cp, SITES), lambda i: (i, 0, 0)), *state_specs],
            out_specs=(*state_specs, pl.BlockSpec((GROUP, cp, SITES), lambda i: (i, 0, 0))),
            compiler_params=pltpu.CompilerParams(vmem_limit_bytes=limit),
            name="creep",
        )(got, chain, micro)
        cells = pl.pallas_call(
            functools.partial(send_back, n_gz, n_gy),
            out_shape=field,
            in_specs=[vm, sm],
            out_specs=vm,
            scratch_shapes=[
                pltpu.VMEM((n * cp, SITES), f32),
                pltpu.SemaphoreType.DMA((n,)),
                pltpu.SemaphoreType.DMA((n,)),
            ],
            compiler_params=pltpu.CompilerParams(
                collective_id=1, has_side_effects=True, vmem_limit_bytes=limit
            ),
            name="send_back",
        )(change, where)
        return cells, chain_after, micro_after

    def lean_tail(got, got_spill):
        where = owner * 256 + flat % cap
        cells, micro_after, chain_after = pl.pallas_call(
            functools.partial(creep_and_return, n_gz, n_gy, cap),
            out_shape=(field, state_shapes[1], state_shapes[0]),
            in_specs=[vm, vm, vm, vm, sm, hbm],
            out_specs=(vm, vm, hbm),
            scratch_shapes=[
                pltpu.VMEM(chain.shape, f32),
                pltpu.VMEM(chain.shape, f32),
                pltpu.VMEM((n, cap, SITES), f32),
                pltpu.VMEM((n, cap, SITES), f32),
                pltpu.SemaphoreType.DMA((n_gz,)),
                pltpu.SemaphoreType.DMA((n_gz,)),
                pltpu.SemaphoreType.DMA((n,)),
                pltpu.SemaphoreType.DMA((n,)),
            ],
            compiler_params=pltpu.CompilerParams(
                collective_id=3, has_side_effects=True, vmem_limit_bytes=limit
            ),
            name="creep_and_return",
        )(got, got_spill, notes_in, micro, where, chain)
        return cells, chain_after, micro_after

    if lean:
        fits_all = jnp.max(notes_in[:, 2, 0]) <= SPILL
        creep_cells, chain_after, micro_after = lax.cond(
            fits_all, lean_tail, dense_tail, *results[5:]
        )
    else:
        creep_cells, chain_after, micro_after = dense_tail()
    return temp, hum, degree_after, creep_cells, chain_after, micro_after


def solution(mesh):
    n_gz, n_gy = mesh.shape["gz"], mesh.shape["gy"]
    cells = P("gz", "gy")
    states = P(("gz", "gy"), None, None)
    tension = P(("gz", "gy"), None)
    return jax.shard_map(
        functools.partial(body, n_gz, n_gy),
        mesh=mesh,
        in_specs=(cells, cells, cells, cells, cells, P(), states, tension),
        out_specs=(cells, cells, cells, cells, states, tension),
        check_vma=False,
    )
```

```python
import functools

import jax
import jax.numpy as jnp
from jax import lax
from jax.experimental import pallas as pl
from jax.experimental.pallas import tpu as pltpu
from jax.sharding import PartitionSpec as P

NX = 48
SITES = 128
KU = 8
SWEEPS = 3
LIFT = 8
PAD = 128
TOP = 8
GROUP = 4
DIRECT = 32
SPILL = 24
DRY = 0.05 + 0.95 / (1.0 + 5.0**16)
MESH = pl.DeviceIdType.MESH


def rate(temp, hum, degree):
    term = 7.5 - 7.5 * hum
    term = term * term
    return 0.05 * (1.0 - degree) * jnp.exp(0.5 * temp) / (1.0 + term * term)


def diffusivity(hum):
    ratio = 5.0 * (1.0 - hum)
    power = ratio * ratio
    power = power * power
    power = power * power
    power = power * power
    return 0.05 + 0.95 / (1.0 + power)


def padded_rows(count):
    return -(-count // 8) * 8


def greet_all(n, n_gy, me):
    barrier = pltpu.get_barrier_semaphore()

    def greet(j, carry):
        other = lax.rem(me + 1 + j, n)
        pl.semaphore_signal(
            barrier, inc=1, device_id=(other // n_gy, lax.rem(other, n_gy)), device_id_type=MESH
        )
        return carry

    lax.fori_loop(0, n - 1, greet, 0)
    pl.semaphore_wait(barrier, n - 1)


def partner(i, n, me):
    return lax.rem(me + 1 + lax.rem(i + n // 2 - 1, n - 1), n)


def sweep_and_send(
    n_gz, n_gy, lean,
    warmth_hbm, moisture_hbm, degree_hbm, tally_hbm, index, spill_index, notes,
    temp_out, hum_out, degree_out, blocks, notes_in, *rest,
):
    if lean:
        got, got_spill = rest[:2]
        rest = rest[2:]
    ext, diff, z_send, z_recv, z_sems, y_sems, note_out, note_in = rest[:8]
    degree, tally, load_sems = rest[8:11]
    if lean:
        send, out_sems, in_sems, own_sems, relay_out, relay_in = rest[11:]
    n = n_gz * n_gy
    rows, cols = degree.shape
    wide = cols + 2 * PAD
    per_row = cols // SITES
    gz = lax.axis_index("gz")
    gy = lax.axis_index("gy")
    me = gz * n_gy + gy
    inner = slice(PAD, PAD + cols)
    body_rows = slice(TOP, TOP + rows)
    loads = [
        pltpu.make_async_copy(warmth_hbm, ext.at[0, 0, body_rows, inner], load_sems.at[0]),
        pltpu.make_async_copy(moisture_hbm, ext.at[0, 1, body_rows, inner], load_sems.at[1]),
        pltpu.make_async_copy(degree_hbm, degree, load_sems.at[2]),
        pltpu.make_async_copy(tally_hbm, tally, load_sems.at[3]),
    ]
    for load in loads:
        load.start()
    greet_all(n, n_gy, me)

    def note_copy(o, at):
        return pltpu.make_async_remote_copy(
            src_ref=notes.at[o],
            dst_ref=notes_in.at[at],
            send_sem=note_out.at[o],
            recv_sem=note_in.at[at],
            device_id=(o // n_gy, lax.rem(o, n_gy)),
            device_id_type=MESH,
        )

    def tell(i, carry):
        note_copy(partner(i, n, me), me).start()
        return carry

    x = lax.rem(lax.broadcasted_iota(jnp.int32, (8, cols), 1), NX)
    has_west = x > 0
    has_east = x < NX - 1
    for load in loads:
        load.wait()

    for s in range(SWEEPS):
        for f in range(2):
            z_send[s, 0, f : f + 1] = ext[s, f, TOP : TOP + 1, inner]
            z_send[s, 1, f : f + 1] = ext[s, f, TOP + rows - 1 : TOP + rows, inner]

        def z_copy(side, s=s):
            to = gz - 1 + 2 * side
            return pltpu.make_async_remote_copy(
                src_ref=z_send.at[s, side],
                dst_ref=z_recv.at[s, 1 - side],
                send_sem=z_sems.at[s, 0, side],
                recv_sem=z_sems.at[s, 1, 1 - side],
                device_id=(to, gy),
                device_id_type=MESH,
            )

        def y_copy(side, s=s):
            to = gy - 1 + 2 * side
            a = PAD if side == 0 else cols
            b = PAD + cols if side == 0 else 0
            return pltpu.make_async_remote_copy(
                src_ref=ext.at[s, :, body_rows, pl.ds(a, PAD)],
                dst_ref=ext.at[s, :, body_rows, pl.ds(b, PAD)],
                send_sem=y_sems.at[s, 0, side],
                recv_sem=y_sems.at[s, 1, 1 - side],
                device_id=(gz, to),
                device_id_type=MESH,
            )

        there = (gz > 0, gz < n_gz - 1)
        beside = (gy > 0, gy < n_gy - 1)
        for side in range(2):
            pl.when(beside[side])(lambda side=side: y_copy(side).start())
            pl.when(there[side])(lambda side=side: z_copy(side).start())

        if s == 0:
            lax.fori_loop(0, n - 1, tell, 0)
            notes_in[me] = notes[me]

        for side in range(2):

            @pl.when(jnp.logical_not(there[side]))
            def _(side=side, s=s):
                z_recv[s, side] = jnp.zeros((2, cols), jnp.float32)

            @pl.when(jnp.logical_not(beside[side]))
            def _(side=side, s=s):
                b = 0 if side == 0 else PAD + cols
                ext[s, :, body_rows, pl.ds(b, PAD)] = jnp.zeros((2, rows, PAD), jnp.float32)

        for side in range(2):
            pl.when(there[side])(lambda side=side: z_copy(1 - side).wait_recv())
            pl.when(beside[side])(lambda side=side: y_copy(1 - side).wait_recv())

        for f in range(2):
            ext[s, f, TOP - 1 : TOP, inner] = z_recv[s, 0, f : f + 1]
            ext[s, f, TOP + rows : TOP + rows + 1, inner] = z_recv[s, 1, f : f + 1]
        diff[TOP - 1 : TOP, inner] = diffusivity(z_recv[s, 0, 1:2])
        diff[TOP + rows : TOP + rows + 1, inner] = diffusivity(z_recv[s, 1, 1:2])
        for r in range(0, rows, 8):
            here = slice(TOP + r, TOP + r + 8)
            diff[here, :] = diffusivity(ext[s, 1, here, :])

        for r in range(0, rows, 8):
            here = slice(TOP + r, TOP + r + 8)
            up = slice(TOP + r + 1, TOP + r + 9)
            down = slice(TOP + r - 1, TOP + r + 7)
            own = slice(r, r + 8)
            temp = ext[s, 0, here, :]
            hum = ext[s, 1, here, :]
            cond = diff[here, :]

            def aside(v, shift):
                return pltpu.roll(v, shift % wide, 1)[:, inner]

            total = (
                ext[s, 0, up, inner] + ext[s, 0, down, inner] + aside(temp, -NX) + aside(temp, NX)
            )
            total = total + jnp.where(has_east, aside(temp, -1), 0.0)
            total = total + jnp.where(has_west, aside(temp, 1), 0.0)
            t0 = temp[:, inner]
            h0 = hum[:, inner]
            d0 = cond[:, inner]
            progress = rate(t0, h0, degree[own, :])
            near = [
                (ext[s, 1, up, inner], diff[up, inner]),
                (ext[s, 1, down, inner], diff[down, inner]),
                (aside(hum, -NX), aside(cond, -NX)),
                (aside(hum, NX), aside(cond, NX)),
                (
                    jnp.where(has_east, aside(hum, -1), 0.0),
                    jnp.where(has_east, aside(cond, -1), DRY),
                ),
                (
                    jnp.where(has_west, aside(hum, 1), 0.0),
                    jnp.where(has_west, aside(cond, 1), DRY),
                ),
            ]
            conduct = None
            inflow = None
            for g, dg in near:
                c = 0.5 * (d0 + dg)
                conduct = c if conduct is None else conduct + c
                inflow = c * g if inflow is None else inflow + c * g
            t1 = (ext[0, 0, here, inner] + 4.0 * progress + total) / 7.0
            h1 = (ext[0, 1, here, inner] - 0.5 * progress + inflow) / (1.0 + conduct)
            if s < SWEEPS - 1:
                ext[s + 1, 0, here, inner] = t1
                ext[s + 1, 1, here, inner] = h1
            else:
                temp_out[own, :] = t1
                hum_out[own, :] = h1
                a1 = degree[own, :] + rate(t1, h1, degree[own, :])
                degree_out[own, :] = a1
                stress = -a1 * (0.5 * t1 + 2.0 * (1.0 - h1))
                phi = jnp.exp(0.3 * t1) * (0.1 + 0.9 * h1 * h1)
                lane = lax.broadcasted_iota(jnp.int32, (8, SITES), 1)
                for j in range(per_row):
                    cut = slice(j * SITES, (j + 1) * SITES)
                    at = slice(j * rows + r, j * rows + r + 8)
                    placed = lane < tally[own, j : j + 1]
                    blocks[0, at, :] = jnp.where(placed, phi[:, cut], 0.0)
                    blocks[1, at, :] = jnp.where(placed, stress[:, cut], 0.0)

    nb = rows * per_row
    blocks[0, nb : nb + 8, :] = jnp.zeros((8, SITES), jnp.float32)
    blocks[1, nb : nb + 8, :] = jnp.zeros((8, SITES), jnp.float32)

    if lean:
        z, x = gz // 2, lax.rem(gz, 2)
        y, core = gy // 2, lax.rem(gy, 2)
        depth = n // 8

        def spill_copy(sem, arrived, base, count, to):
            part = got_spill.at[pl.ds(base, count)]
            return pltpu.make_async_remote_copy(
                src_ref=part,
                dst_ref=part,
                send_sem=relay_out.at[sem],
                recv_sem=relay_in.at[arrived],
                device_id=to,
                device_id_type=MESH,
            )

        line = (core * 4 + x * 2 + y) * depth
        for l in range(SPILL):
            k = spill_index[l]
            got_spill[line + z, l : l + 1, :] = blocks[0, pl.ds(k, 1), :]
            got_spill[line + z, SPILL + l : SPILL + l + 1, :] = blocks[1, pl.ds(k, 1), :]

        def z_other(d):
            return lax.rem(z + d, depth)

        for d in range(1, depth):
            spill_copy(d, depth - d, line + z, 1, (z_other(d) * 2 + x, gy)).start()

        def fill(o):
            for l in range(DIRECT):
                k = index[o * DIRECT + l]
                send[o, l : l + 1, :] = blocks[0, pl.ds(k, 1), :]
                send[o, DIRECT + l : DIRECT + l + 1, :] = blocks[1, pl.ds(k, 1), :]

        def row_copy(o, at):
            return pltpu.make_async_remote_copy(
                src_ref=send.at[o],
                dst_ref=got.at[at],
                send_sem=out_sems.at[o],
                recv_sem=in_sems.at[at],
                device_id=(o // n_gy, lax.rem(o, n_gy)),
                device_id_type=MESH,
            )

        def push(i, carry):
            o = partner(i, n, me)
            fill(o)
            row_copy(o, me).start()
            return carry

        lax.fori_loop(0, n - 1, push, 0)
        fill(me)
        own_copy = pltpu.make_async_copy(send.at[me], got.at[me], own_sems)
        own_copy.start()

        for d in range(1, depth):
            spill_copy(d, depth - d, line + z_other(d), 1, (z_other(d) * 2 + x, gy)).wait_recv()
        spill_copy(depth, depth, line, depth, (gz, (1 - y) * 2 + core)).start()
        other = (core * 4 + x * 2 + 1 - y) * depth
        spill_copy(depth, depth, other, depth, (gz, (1 - y) * 2 + core)).wait_recv()
        pair = (core * 4 + x * 2) * depth
        spill_copy(depth + 1, depth + 1, pair, 2 * depth, (z * 2 + 1 - x, gy)).start()
        other = (core * 4 + (1 - x) * 2) * depth
        spill_copy(depth + 1, depth + 1, other, 2 * depth, (z * 2 + 1 - x, gy)).wait_recv()
        half = core * 4 * depth
        spill_copy(depth + 2, depth + 2, half, 4 * depth, (gz, y * 2 + 1 - core)).start()
        other = (1 - core) * 4 * depth
        spill_copy(depth + 2, depth + 2, other, 4 * depth, (gz, y * 2 + 1 - core)).wait_recv()

        for d in range(1, depth):
            spill_copy(d, depth - d, line + z, 1, (z_other(d) * 2 + x, gy)).wait_send()
        spill_copy(depth, depth, line, depth, (gz, (1 - y) * 2 + core)).wait_send()
        spill_copy(depth + 1, depth + 1, pair, 2 * depth, (z * 2 + 1 - x, gy)).wait_send()
        spill_copy(depth + 2, depth + 2, half, 4 * depth, (gz, y * 2 + 1 - core)).wait_send()

    for s in range(SWEEPS):
        for side in range(2):
            a = PAD if side == 0 else cols
            pl.when((gz > 0, gz < n_gz - 1)[side])(
                lambda s=s, side=side: pltpu.make_async_remote_copy(
                    src_ref=z_send.at[s, side],
                    dst_ref=z_recv.at[s, 1 - side],
                    send_sem=z_sems.at[s, 0, side],
                    recv_sem=z_sems.at[s, 1, 1 - side],
                    device_id=(gz - 1 + 2 * side, gy),
                    device_id_type=MESH,
                ).wait_send()
            )
            pl.when((gy > 0, gy < n_gy - 1)[side])(
                lambda s=s, side=side, a=a: pltpu.make_async_remote_copy(
                    src_ref=ext.at[s, :, body_rows, pl.ds(a, PAD)],
                    dst_ref=ext.at[s, :, body_rows, pl.ds(a, PAD)],
                    send_sem=y_sems.at[s, 0, side],
                    recv_sem=y_sems.at[s, 1, 1 - side],
                    device_id=(gz, gy - 1 + 2 * side),
                    device_id_type=MESH,
                ).wait_send()
            )

    def told(i, carry):
        o = partner(i, n, me)
        note_copy(o, o).wait()
        return carry

    lax.fori_loop(0, n - 1, told, 0)

    if lean:
        own_copy.wait()

        def finish(i, carry):
            o = partner(i, n, me)
            row_copy(o, o).wait()
            return carry

        lax.fori_loop(0, n - 1, finish, 0)


def send_dense(
    n_gz, n_gy, cap, blocks, index, solid, got, send, out_sems, in_sems, own_sem
):
    n = n_gz * n_gy
    cp = padded_rows(cap + 1)
    me = lax.axis_index("gz") * n_gy + lax.axis_index("gy")
    greet_all(n, n_gy, me)

    def row_copy(o, at):
        return pltpu.make_async_remote_copy(
            src_ref=send.at[o],
            dst_ref=got.at[at],
            send_sem=out_sems.at[o],
            recv_sem=in_sems.at[at],
            device_id=(o // n_gy, lax.rem(o, n_gy)),
            device_id_type=MESH,
        )

    def fill(o):
        for l in range(cap):
            k = index[o * cap + l]
            send[o, l : l + 1, :] = blocks[0, pl.ds(k, 1), :]
            send[o, cp + l : cp + l + 1, :] = blocks[1, pl.ds(k, 1), :]
        send[o, cap : cap + 1, :] = solid[pl.ds(o, 1), :]

    def push(i, carry):
        o = partner(i, n, me)
        fill(o)
        row_copy(o, me).start()
        return carry

    lax.fori_loop(0, n - 1, push, 0)
    fill(me)
    own_copy = pltpu.make_async_copy(send.at[me], got.at[me], own_sem)
    own_copy.start()
    own_copy.wait()

    def finish(i, carry):
        o = partner(i, n, me)
        row_copy(o, o).wait()
        return carry

    lax.fori_loop(0, n - 1, finish, 0)


def creep(cap, got, chain, micro, chain_out, micro_out, change):
    cp = padded_rows(cap + 1)
    unit = lax.broadcasted_iota(jnp.int32, (KU, SITES), 0)
    speed = jnp.full((KU, SITES), -10.0, jnp.float32)
    for m in range(1, KU):
        speed = jnp.where(unit == m, -10.0 / 3.0**m, speed)
    sub = lax.broadcasted_iota(jnp.int32, (cap, SITES), 0)
    lane = lax.broadcasted_iota(jnp.int32, (cap, SITES), 1)
    for q in range(GROUP):
        base = q * cap
        phi = got[q, 0:cap, :]
        stress = got[q, cp : cp + cap, :]
        row = got[q, cap : cap + 1, :]
        solid = jnp.sum(jnp.where(sub == lane, row, 0.0), axis=1, keepdims=True)
        s0 = micro[base : base + cap, :]
        s1 = s0 / (1.0 + 0.2 * phi * s0)
        micro_out[base : base + cap, :] = s1
        flow = 0.1 * phi * s1 * stress
        for l0 in range(0, cap, 8):
            l1 = min(l0 + 8, cap)
            old = chain[base + l0 : base + l1]
            decay = jnp.exp(phi[l0:l1][:, None, :] * speed[None])
            new = decay * old + 0.15 * (1.0 - decay) * stress[l0:l1][:, None, :]
            chain_out[base + l0 : base + l1] = new
            kelvin = jnp.sum(new - old, axis=1)
            change[q, l0:l1, :] = solid[l0:l1] * kelvin + flow[l0:l1]
        change[q, cap:cp, :] = jnp.zeros((cp - cap, SITES), jnp.float32)


def creep_and_return(
    n_gz, n_gy, cap,
    got, spill, notes, micro, where, chain,
    out, micro_out, chain_out,
    old_state, new_state, change, back, read_sems, write_sems, out_sems, in_sems,
):
    n = n_gz * n_gy
    depth = n // 8
    rows, cols = out.shape
    gz = lax.axis_index("gz")
    gy = lax.axis_index("gy")
    me = gz * n_gy + gy
    held = DIRECT + SPILL
    part = n_gy * cap

    def read(g):
        at = pl.ds(g * part, part)
        return pltpu.make_async_copy(chain.at[at], old_state.at[at], read_sems.at[g])

    def write(g):
        at = pl.ds(g * part, part)
        return pltpu.make_async_copy(new_state.at[at], chain_out.at[at], write_sems.at[g])

    def turn(i):
        mid = n_gz // 2
        return lax.rem(gz // mid + 1 + i // mid, 2) * mid + lax.rem(gz + i, mid)

    def begin(i, carry):
        read(turn(i)).start()
        return carry

    lax.fori_loop(0, n_gz, begin, 0)
    greet_all(n, n_gy, me)

    unit = lax.broadcasted_iota(jnp.int32, (KU, SITES), 0)
    speed = jnp.full((KU, SITES), -10.0, jnp.float32)
    for m in range(1, KU):
        speed = jnp.where(unit == m, -10.0 / 3.0**m, speed)
    tall = -(-cap // 16) * 16
    sub = lax.broadcasted_iota(jnp.int32, (tall, SITES), 0)
    lane = lax.broadcasted_iota(jnp.int32, (tall, SITES), 1)
    row_id = lax.rem(lax.broadcasted_iota(jnp.int32, (tall, 3 * held), 1), held)
    row_id = row_id.astype(jnp.float32)

    def row_copy(o, at):
        return pltpu.make_async_remote_copy(
            src_ref=change.at[o],
            dst_ref=back.at[at],
            send_sem=out_sems.at[o],
            recv_sem=in_sems.at[at],
            device_id=(o // n_gy, lax.rem(o, n_gy)),
            device_id_type=MESH,
        )

    def group(i, carry):
        g = turn(i)
        read(g).wait()
        start = pl.multiple_of(g * part, 8)
        s0 = micro[pl.ds(start, part), :]
        z, x = g // 2, lax.rem(g, 2)
        all_phi = []
        all_stress = []
        all_solid = []
        for q in range(n_gy):
            o = g * n_gy + q
            place = (q % 2 * 4 + x * 2 + q // 2) * depth + z

            def column(r):
                row = notes[o, r : r + 1, :]
                return jnp.sum(jnp.where(sub == lane, row, 0.0), axis=1, keepdims=True)

            pick = jnp.where(column(0) == row_id, 1.0, 0.0).astype(jnp.bfloat16)
            all_solid.append(column(1)[:cap])
            rows_phi = jnp.concatenate([got[o, 0:DIRECT, :], spill[place, 0:SPILL, :]], axis=0)
            rows_stress = jnp.concatenate(
                [got[o, DIRECT : 2 * DIRECT, :], spill[place, SPILL : 2 * SPILL, :]], axis=0
            )
            both = jnp.concatenate([rows_phi, rows_stress], axis=1)
            high = both.astype(jnp.bfloat16)
            left = both - high.astype(jnp.float32)
            middle = left.astype(jnp.bfloat16)
            low = (left - middle.astype(jnp.float32)).astype(jnp.bfloat16)
            parts = jnp.concatenate([high, middle, low], axis=0)
            both = jnp.dot(pick, parts, preferred_element_type=jnp.float32)
            all_phi.append(both[:cap, :SITES])
            all_stress.append(both[:cap, SITES:])
        phis = jnp.concatenate(all_phi, axis=0)
        s1 = s0 / (1.0 + 0.2 * phis * s0)
        micro_out[pl.ds(start, part), :] = s1
        for q in range(n_gy):
            o = g * n_gy + q
            phi, stress, solid = all_phi[q], all_stress[q], all_solid[q]
            flow = 0.1 * phi * s1[q * cap : (q + 1) * cap] * stress
            base = g * part + q * cap
            for l0 in range(0, cap, 8):
                l1 = min(l0 + 8, cap)
                at = pl.ds(base + l0, l1 - l0)
                old = old_state[at]
                decay = jnp.exp(phi[l0:l1][:, None, :] * speed[None])
                new = decay * old + 0.15 * (1.0 - decay) * stress[l0:l1][:, None, :]
                new_state[at] = new
                kelvin = jnp.sum(new - old, axis=1)
                change[o, l0:l1, :] = solid[l0:l1] * kelvin + flow[l0:l1]
            pl.when(o != me)(lambda o=o: row_copy(o, me).start())
        write(g).start()
        return carry

    lax.fori_loop(0, n_gz, group, 0)
    back[me] = change[me]

    def finish(i, carry):
        o = partner(i, n, me)
        row_copy(o, o).wait()
        return carry

    lax.fori_loop(0, n - 1, finish, 0)
    per_row = cols // SITES

    def place_cells(g, carry):
        r = pl.multiple_of(g * 8, 8)
        for j in range(per_row):
            lines = []
            for k in range(8):
                w = where[(r + k) * per_row + j]
                lines.append(back[w // 256, pl.ds(lax.rem(w, 256), 1), :])
            out[pl.ds(r, 8), j * SITES : (j + 1) * SITES] = jnp.concatenate(lines, axis=0)
        return carry

    lax.fori_loop(0, rows // 8, place_cells, 0)

    def end(i, carry):
        write(turn(i)).wait()
        return carry

    lax.fori_loop(0, n_gz, end, 0)


def send_back(n_gz, n_gy, change, where, out, back, out_sems, in_sems):
    n = n_gz * n_gy
    rows, cols = out.shape
    cp = change.shape[1]
    me = lax.axis_index("gz") * n_gy + lax.axis_index("gy")
    greet_all(n, n_gy, me)

    def push(i, carry):
        o = partner(i, n, me)
        pltpu.make_async_remote_copy(
            src_ref=change.at[o],
            dst_ref=back.at[pl.ds(pl.multiple_of(me * cp, 8), cp)],
            send_sem=out_sems.at[o],
            recv_sem=in_sems.at[me],
            device_id=(o // n_gy, lax.rem(o, n_gy)),
            device_id_type=MESH,
        ).start()
        return carry

    lax.fori_loop(0, n - 1, push, 0)
    back[pl.ds(pl.multiple_of(me * cp, 8), cp), :] = change[me]

    def finish(i, carry):
        o = partner(i, n, me)
        pltpu.make_async_remote_copy(
            src_ref=change.at[o],
            dst_ref=back.at[pl.ds(pl.multiple_of(o * cp, 8), cp)],
            send_sem=out_sems.at[o],
            recv_sem=in_sems.at[o],
            device_id=(o // n_gy, lax.rem(o, n_gy)),
            device_id_type=MESH,
        ).wait()
        return carry

    lax.fori_loop(0, n - 1, finish, 0)
    per_row = cols // SITES

    def place(g, carry):
        r = pl.multiple_of(g * 8, 8)
        for j in range(per_row):
            lines = [back[pl.ds(where[(r + k) * per_row + j], 1), :] for k in range(8)]
            out[pl.ds(r, 8), j * SITES : (j + 1) * SITES] = jnp.concatenate(lines, axis=0)
        return carry

    lax.fori_loop(0, rows // 8, place, 0)


def body(n_gz, n_gy, warmth, moisture, degree, tally, keeper, pouring, chain, micro):
    n = n_gz * n_gy
    rows, cols = warmth.shape
    per_row = cols // SITES
    slots = chain.shape[0]
    cap = slots // n
    cp = padded_rows(cap + 1)
    nb = rows * per_row
    lifts = rows // LIFT
    vm = pl.BlockSpec(memory_space=pltpu.VMEM)
    sm = pl.BlockSpec(memory_space=pltpu.SMEM)
    hbm = pl.BlockSpec(memory_space=pl.ANY)
    far = pl.BlockSpec(memory_space=pltpu.HBM)
    f32 = jnp.float32

    local_times = lax.dynamic_slice_in_dim(pouring, lax.axis_index("gz") * lifts, lifts)
    age = 2400.0 - jnp.repeat(local_times, LIFT).astype(f32)
    solid = jnp.sqrt(600.0 / age) + 0.2
    flat = keeper.reshape(-1)
    slot_id = jnp.arange(slots, dtype=jnp.int32)
    hit = flat[None, :] == slot_id[:, None]
    block = jnp.arange(nb, dtype=jnp.int32)
    held = (block % per_row) * rows + block // per_row
    solid_slot = jnp.sum(jnp.where(hit, jnp.repeat(solid, per_row)[None, :], 0.0), axis=1)
    solid_rows = jnp.pad(solid_slot.reshape(n, cap), ((0, 0), (0, SITES - cap)))
    lean = cap >= DIRECT + 8 and n % 8 == 0 and n_gy == 4 and GROUP * cap % 8 == 0
    owner = flat // cap
    earlier = flat[None, :] < flat[:, None]
    if lean:
        rank = jnp.sum(earlier & (owner[None, :] == owner[:, None]), axis=1, dtype=jnp.int32)
        over = rank >= DIRECT
        spot = jnp.sum(earlier & over[None, :], axis=1, dtype=jnp.int32)
        spilled = jnp.sum(over, dtype=jnp.int32)
        code = jnp.where(over, DIRECT + spot, rank)
        slot_map = jnp.sum(jnp.where(hit, code[None, :] + 1, 0), axis=1) - 1
        target = jnp.where(over, n * DIRECT + spot, owner * DIRECT + rank)
        line_id = jnp.arange(n * DIRECT + SPILL, dtype=jnp.int32)
        fits = target[None, :] == line_id[:, None]
        index = nb + jnp.sum(jnp.where(fits, held[None, :] - nb, 0), axis=1)
        index, spill_index = index[: n * DIRECT], index[n * DIRECT :]
        slot_map = jnp.pad(slot_map.reshape(n, cap).astype(f32), ((0, 0), (0, SITES - cap)))
        count = jnp.broadcast_to(spilled.astype(f32), (n, SITES))
        notes = [slot_map, solid_rows, count]
    else:
        index = spill_index = jnp.zeros((8,), jnp.int32)
        notes = [solid_rows, solid_rows, solid_rows]
    notes = jnp.stack(notes + [jnp.zeros((n, SITES), f32)] * 5, axis=1)

    field = jax.ShapeDtypeStruct((rows, cols), f32)
    outs = [field, field, field, jax.ShapeDtypeStruct((2, nb + 8, SITES), f32)]
    outs += [jax.ShapeDtypeStruct((n, 8, SITES), f32)]
    scratch = [
        pltpu.VMEM((SWEEPS, 2, rows + 2 * TOP, cols + 2 * PAD), f32),
        pltpu.VMEM((rows + 2 * TOP, cols + 2 * PAD), f32),
        pltpu.VMEM((SWEEPS, 2, 2, cols), f32),
        pltpu.VMEM((SWEEPS, 2, 2, cols), f32),
        pltpu.SemaphoreType.DMA((SWEEPS, 2, 2)),
        pltpu.SemaphoreType.DMA((SWEEPS, 2, 2)),
        pltpu.SemaphoreType.DMA((n,)),
        pltpu.SemaphoreType.DMA((n,)),
        pltpu.VMEM((rows, cols), f32),
        pltpu.VMEM((rows, per_row), jnp.int32),
        pltpu.SemaphoreType.DMA((4,)),
    ]
    out_specs = [vm] * 5
    if lean:
        outs += [jax.ShapeDtypeStruct((n, 2 * DIRECT, SITES), f32)]
        outs += [jax.ShapeDtypeStruct((n, 2 * SPILL, SITES), f32)]
        out_specs += [hbm, vm]
        scratch += [
            pltpu.VMEM((n, 2 * DIRECT, SITES), f32),
            pltpu.SemaphoreType.DMA((n,)),
            pltpu.SemaphoreType.DMA((n,)),
            pltpu.SemaphoreType.DMA,
            pltpu.SemaphoreType.DMA((n // 8 + 3,)),
            pltpu.SemaphoreType.DMA((n // 8 + 3,)),
        ]
    limit = 40 * 1024 * 1024
    results = pl.pallas_call(
        functools.partial(sweep_and_send, n_gz, n_gy, lean),
        out_shape=tuple(outs),
        in_specs=[far, far, far, far, sm, sm, vm],
        out_specs=tuple(out_specs),
        scratch_shapes=scratch,
        compiler_params=pltpu.CompilerParams(
            collective_id=0, has_side_effects=True, vmem_limit_bytes=60 * 1024 * 1024
        ),
        name="sweep_and_send",
    )(warmth, moisture, degree, tally, index, spill_index, notes)
    temp, hum, degree_after, blocks, notes_in = results[:5]

    state_specs = (
        pl.BlockSpec((GROUP * cap, KU, SITES), lambda i: (i, 0, 0)),
        pl.BlockSpec((GROUP * cap, SITES), lambda i: (i, 0)),
    )
    state_shapes = (
        jax.ShapeDtypeStruct(chain.shape, f32),
        jax.ShapeDtypeStruct(micro.shape, f32),
    )

    def dense_tail(*_):
        held_there = flat[None, :] == slot_id[:, None]
        index = nb + jnp.sum(jnp.where(held_there, held[None, :] - nb, 0), axis=1)
        where = (flat // cap) * cp + flat % cap
        got = pl.pallas_call(
            functools.partial(send_dense, n_gz, n_gy, cap),
            out_shape=jax.ShapeDtypeStruct((n, 2 * cp, SITES), f32),
            in_specs=[vm, sm, vm],
            out_specs=hbm,
            scratch_shapes=[
                pltpu.VMEM((n, 2 * cp, SITES), f32),
                pltpu.SemaphoreType.DMA((n,)),
                pltpu.SemaphoreType.DMA((n,)),
                pltpu.SemaphoreType.DMA,
            ],
            compiler_params=pltpu.CompilerParams(
                collective_id=2, has_side_effects=True, vmem_limit_bytes=limit
            ),
            name="send_dense",
        )(blocks, index, solid_rows)
        chain_after, micro_after, change = pl.pallas_call(
            functools.partial(creep, cap),
            grid=(n // GROUP,),
            out_shape=state_shapes + (jax.ShapeDtypeStruct((n, cp, SITES), f32),),
            in_specs=[pl.BlockSpec((GROUP, 2 * cp, SITES), lambda i: (i, 0, 0)), *state_specs],
            out_specs=(*state_specs, pl.BlockSpec((GROUP, cp, SITES), lambda i: (i, 0, 0))),
            compiler_params=pltpu.CompilerParams(vmem_limit_bytes=limit),
            name="creep",
        )(got, chain, micro)
        cells = pl.pallas_call(
            functools.partial(send_back, n_gz, n_gy),
            out_shape=field,
            in_specs=[vm, sm],
            out_specs=vm,
            scratch_shapes=[
                pltpu.VMEM((n * cp, SITES), f32),
                pltpu.SemaphoreType.DMA((n,)),
                pltpu.SemaphoreType.DMA((n,)),
            ],
            compiler_params=pltpu.CompilerParams(
                collective_id=1, has_side_effects=True, vmem_limit_bytes=limit
            ),
            name="send_back",
        )(change, where)
        return cells, chain_after, micro_after

    def lean_tail(got, got_spill):
        where = owner * 256 + flat % cap
        cells, micro_after, chain_after = pl.pallas_call(
            functools.partial(creep_and_return, n_gz, n_gy, cap),
            out_shape=(field, state_shapes[1], state_shapes[0]),
            in_specs=[vm, vm, vm, vm, sm, hbm],
            out_specs=(vm, vm, hbm),
            scratch_shapes=[
                pltpu.VMEM(chain.shape, f32),
                pltpu.VMEM(chain.shape, f32),
                pltpu.VMEM((n, cap, SITES), f32),
                pltpu.VMEM((n, cap, SITES), f32),
                pltpu.SemaphoreType.DMA((n_gz,)),
                pltpu.SemaphoreType.DMA((n_gz,)),
                pltpu.SemaphoreType.DMA((n,)),
                pltpu.SemaphoreType.DMA((n,)),
            ],
            compiler_params=pltpu.CompilerParams(
                collective_id=3, has_side_effects=True, vmem_limit_bytes=limit
            ),
            name="creep_and_return",
        )(got, got_spill, notes_in, micro, where, chain)
        return cells, chain_after, micro_after

    if lean:
        fits_all = jnp.max(notes_in[:, 2, 0]) <= SPILL
        creep_cells, chain_after, micro_after = lax.cond(
            fits_all, lean_tail, dense_tail, *results[5:]
        )
    else:
        creep_cells, chain_after, micro_after = dense_tail()
    return temp, hum, degree_after, creep_cells, chain_after, micro_after


def solution(mesh):
    n_gz, n_gy = mesh.shape["gz"], mesh.shape["gy"]
    cells = P("gz", "gy")
    states = P(("gz", "gy"), None, None)
    tension = P(("gz", "gy"), None)
    return jax.shard_map(
        functools.partial(body, n_gz, n_gy),
        mesh=mesh,
        in_specs=(cells, cells, cells, cells, cells, P(), states, tension),
        out_specs=(cells, cells, cells, cells, states, tension),
        check_vma=False,
    )
```

```python
import functools

import jax
import jax.numpy as jnp
from jax import lax
from jax.experimental import pallas as pl
from jax.experimental.pallas import tpu as pltpu
from jax.sharding import PartitionSpec as P

NX = 48
SITES = 128
KU = 8
SWEEPS = 3
LIFT = 8
PAD = 128
TOP = 8
GROUP = 4
DIRECT = 24
SPILL = 40
DRY = 0.05 + 0.95 / (1.0 + 5.0**16)
MESH = pl.DeviceIdType.MESH


def rate(temp, hum, degree):
    term = 7.5 - 7.5 * hum
    term = term * term
    return 0.05 * (1.0 - degree) * jnp.exp(0.5 * temp) / (1.0 + term * term)


def diffusivity(hum):
    ratio = 5.0 * (1.0 - hum)
    power = ratio * ratio
    power = power * power
    power = power * power
    power = power * power
    return 0.05 + 0.95 / (1.0 + power)


def padded_rows(count):
    return -(-count // 8) * 8


def greet_all(n, n_gy, me):
    barrier = pltpu.get_barrier_semaphore()

    def greet(j, carry):
        other = lax.rem(me + 1 + j, n)
        pl.semaphore_signal(
            barrier, inc=1, device_id=(other // n_gy, lax.rem(other, n_gy)), device_id_type=MESH
        )
        return carry

    lax.fori_loop(0, n - 1, greet, 0)
    pl.semaphore_wait(barrier, n - 1)


def partner(i, n, me):
    return lax.rem(me + 1 + lax.rem(i + n // 2 - 1, n - 1), n)


def sweep_and_send(
    n_gz, n_gy, lean,
    warmth_hbm, moisture_hbm, degree_hbm, tally_hbm, index, notes,
    temp_out, hum_out, degree_out, blocks, notes_in, *rest,
):
    if lean:
        got, got_spill = rest[:2]
        rest = rest[2:]
    ext, diff, z_send, z_recv, z_sems, y_sems, note_out, note_in = rest[:8]
    degree, tally, load_sems = rest[8:11]
    if lean:
        send, out_sems, in_sems, own_sems, relay_out, relay_in = rest[11:]
    n = n_gz * n_gy
    rows, cols = degree.shape
    wide = cols + 2 * PAD
    per_row = cols // SITES
    gz = lax.axis_index("gz")
    gy = lax.axis_index("gy")
    me = gz * n_gy + gy
    inner = slice(PAD, PAD + cols)
    body_rows = slice(TOP, TOP + rows)
    loads = [
        pltpu.make_async_copy(warmth_hbm, ext.at[0, 0, body_rows, inner], load_sems.at[0]),
        pltpu.make_async_copy(moisture_hbm, ext.at[0, 1, body_rows, inner], load_sems.at[1]),
        pltpu.make_async_copy(degree_hbm, degree, load_sems.at[2]),
        pltpu.make_async_copy(tally_hbm, tally, load_sems.at[3]),
    ]
    for load in loads:
        load.start()
    greet_all(n, n_gy, me)

    def note_copy(o, at):
        return pltpu.make_async_remote_copy(
            src_ref=notes.at[o],
            dst_ref=notes_in.at[at],
            send_sem=note_out.at[o],
            recv_sem=note_in.at[at],
            device_id=(o // n_gy, lax.rem(o, n_gy)),
            device_id_type=MESH,
        )

    def tell(i, carry):
        note_copy(partner(i, n, me), me).start()
        return carry

    x = lax.rem(lax.broadcasted_iota(jnp.int32, (8, cols), 1), NX)
    has_west = x > 0
    has_east = x < NX - 1
    for load in loads:
        load.wait()

    for s in range(SWEEPS):
        for f in range(2):
            z_send[s, 0, f : f + 1] = ext[s, f, TOP : TOP + 1, inner]
            z_send[s, 1, f : f + 1] = ext[s, f, TOP + rows - 1 : TOP + rows, inner]

        def z_copy(side, s=s):
            to = gz - 1 + 2 * side
            return pltpu.make_async_remote_copy(
                src_ref=z_send.at[s, side],
                dst_ref=z_recv.at[s, 1 - side],
                send_sem=z_sems.at[s, 0, side],
                recv_sem=z_sems.at[s, 1, 1 - side],
                device_id=(to, gy),
                device_id_type=MESH,
            )

        def y_copy(side, s=s):
            to = gy - 1 + 2 * side
            a = PAD if side == 0 else cols
            b = PAD + cols if side == 0 else 0
            return pltpu.make_async_remote_copy(
                src_ref=ext.at[s, :, body_rows, pl.ds(a, PAD)],
                dst_ref=ext.at[s, :, body_rows, pl.ds(b, PAD)],
                send_sem=y_sems.at[s, 0, side],
                recv_sem=y_sems.at[s, 1, 1 - side],
                device_id=(gz, to),
                device_id_type=MESH,
            )

        there = (gz > 0, gz < n_gz - 1)
        beside = (gy > 0, gy < n_gy - 1)
        for side in range(2):
            pl.when(beside[side])(lambda side=side: y_copy(side).start())
            pl.when(there[side])(lambda side=side: z_copy(side).start())

        if s == 0:
            lax.fori_loop(0, n - 1, tell, 0)
            notes_in[me] = notes[me]

        for side in range(2):

            @pl.when(jnp.logical_not(there[side]))
            def _(side=side, s=s):
                z_recv[s, side] = jnp.zeros((2, cols), jnp.float32)

            @pl.when(jnp.logical_not(beside[side]))
            def _(side=side, s=s):
                b = 0 if side == 0 else PAD + cols
                ext[s, :, body_rows, pl.ds(b, PAD)] = jnp.zeros((2, rows, PAD), jnp.float32)

        for side in range(2):
            pl.when(there[side])(lambda side=side: z_copy(1 - side).wait_recv())
            pl.when(beside[side])(lambda side=side: y_copy(1 - side).wait_recv())

        for f in range(2):
            ext[s, f, TOP - 1 : TOP, inner] = z_recv[s, 0, f : f + 1]
            ext[s, f, TOP + rows : TOP + rows + 1, inner] = z_recv[s, 1, f : f + 1]
        diff[TOP - 1 : TOP, inner] = diffusivity(z_recv[s, 0, 1:2])
        diff[TOP + rows : TOP + rows + 1, inner] = diffusivity(z_recv[s, 1, 1:2])
        for r in range(0, rows, 8):
            here = slice(TOP + r, TOP + r + 8)
            diff[here, :] = diffusivity(ext[s, 1, here, :])

        for r in range(0, rows, 8):
            here = slice(TOP + r, TOP + r + 8)
            up = slice(TOP + r + 1, TOP + r + 9)
            down = slice(TOP + r - 1, TOP + r + 7)
            own = slice(r, r + 8)
            temp = ext[s, 0, here, :]
            hum = ext[s, 1, here, :]
            cond = diff[here, :]

            def aside(v, shift):
                return pltpu.roll(v, shift % wide, 1)[:, inner]

            total = (
                ext[s, 0, up, inner] + ext[s, 0, down, inner] + aside(temp, -NX) + aside(temp, NX)
            )
            total = total + jnp.where(has_east, aside(temp, -1), 0.0)
            total = total + jnp.where(has_west, aside(temp, 1), 0.0)
            t0 = temp[:, inner]
            h0 = hum[:, inner]
            d0 = cond[:, inner]
            progress = rate(t0, h0, degree[own, :])
            near = [
                (ext[s, 1, up, inner], diff[up, inner]),
                (ext[s, 1, down, inner], diff[down, inner]),
                (aside(hum, -NX), aside(cond, -NX)),
                (aside(hum, NX), aside(cond, NX)),
                (
                    jnp.where(has_east, aside(hum, -1), 0.0),
                    jnp.where(has_east, aside(cond, -1), DRY),
                ),
                (
                    jnp.where(has_west, aside(hum, 1), 0.0),
                    jnp.where(has_west, aside(cond, 1), DRY),
                ),
            ]
            conduct = None
            inflow = None
            for g, dg in near:
                c = 0.5 * (d0 + dg)
                conduct = c if conduct is None else conduct + c
                inflow = c * g if inflow is None else inflow + c * g
            t1 = (ext[0, 0, here, inner] + 4.0 * progress + total) / 7.0
            h1 = (ext[0, 1, here, inner] - 0.5 * progress + inflow) / (1.0 + conduct)
            if s < SWEEPS - 1:
                ext[s + 1, 0, here, inner] = t1
                ext[s + 1, 1, here, inner] = h1
            else:
                temp_out[own, :] = t1
                hum_out[own, :] = h1
                a1 = degree[own, :] + rate(t1, h1, degree[own, :])
                degree_out[own, :] = a1
                stress = -a1 * (0.5 * t1 + 2.0 * (1.0 - h1))
                phi = jnp.exp(0.3 * t1) * (0.1 + 0.9 * h1 * h1)
                lane = lax.broadcasted_iota(jnp.int32, (8, SITES), 1)
                for j in range(per_row):
                    cut = slice(j * SITES, (j + 1) * SITES)
                    at = slice(j * rows + r, j * rows + r + 8)
                    placed = lane < tally[own, j : j + 1]
                    blocks[0, at, :] = jnp.where(placed, phi[:, cut], 0.0)
                    blocks[1, at, :] = jnp.where(placed, stress[:, cut], 0.0)

    nb = rows * per_row
    blocks[0, nb : nb + 8, :] = jnp.zeros((8, SITES), jnp.float32)
    blocks[1, nb : nb + 8, :] = jnp.zeros((8, SITES), jnp.float32)

    if lean:
        z, x = gz // 2, lax.rem(gz, 2)
        y, core = gy // 2, lax.rem(gy, 2)
        depth = n // 8

        def spill_copy(sem, arrived, base, count, to):
            part = got_spill.at[pl.ds(base, count)]
            return pltpu.make_async_remote_copy(
                src_ref=part,
                dst_ref=part,
                send_sem=relay_out.at[sem],
                recv_sem=relay_in.at[arrived],
                device_id=to,
                device_id_type=MESH,
            )

        line = (core * 4 + x * 2 + y) * depth
        for l in range(SPILL):
            k = index[n * DIRECT + l]
            got_spill[line + z, l : l + 1, :] = blocks[0, pl.ds(k, 1), :]
            got_spill[line + z, SPILL + l : SPILL + l + 1, :] = blocks[1, pl.ds(k, 1), :]

        def z_other(d):
            return lax.rem(z + d, depth)

        for d in range(1, depth):
            spill_copy(d, depth - d, line + z, 1, (z_other(d) * 2 + x, gy)).start()

        def fill(o):
            for l in range(DIRECT):
                k = index[o * DIRECT + l]
                send[o, l : l + 1, :] = blocks[0, pl.ds(k, 1), :]
                send[o, DIRECT + l : DIRECT + l + 1, :] = blocks[1, pl.ds(k, 1), :]

        def row_copy(o, at):
            return pltpu.make_async_remote_copy(
                src_ref=send.at[o],
                dst_ref=got.at[at],
                send_sem=out_sems.at[o],
                recv_sem=in_sems.at[at],
                device_id=(o // n_gy, lax.rem(o, n_gy)),
                device_id_type=MESH,
            )

        def push(i, carry):
            o = partner(i, n, me)
            fill(o)
            row_copy(o, me).start()
            return carry

        lax.fori_loop(0, n - 1, push, 0)
        fill(me)
        own_copy = pltpu.make_async_copy(send.at[me], got.at[me], own_sems)
        own_copy.start()

        for d in range(1, depth):
            spill_copy(d, depth - d, line + z_other(d), 1, (z_other(d) * 2 + x, gy)).wait_recv()
        spill_copy(depth, depth, line, depth, (gz, (1 - y) * 2 + core)).start()
        other = (core * 4 + x * 2 + 1 - y) * depth
        spill_copy(depth, depth, other, depth, (gz, (1 - y) * 2 + core)).wait_recv()
        pair = (core * 4 + x * 2) * depth
        spill_copy(depth + 1, depth + 1, pair, 2 * depth, (z * 2 + 1 - x, gy)).start()
        other = (core * 4 + (1 - x) * 2) * depth
        spill_copy(depth + 1, depth + 1, other, 2 * depth, (z * 2 + 1 - x, gy)).wait_recv()
        half = core * 4 * depth
        spill_copy(depth + 2, depth + 2, half, 4 * depth, (gz, y * 2 + 1 - core)).start()
        other = (1 - core) * 4 * depth
        spill_copy(depth + 2, depth + 2, other, 4 * depth, (gz, y * 2 + 1 - core)).wait_recv()

        for d in range(1, depth):
            spill_copy(d, depth - d, line + z, 1, (z_other(d) * 2 + x, gy)).wait_send()
        spill_copy(depth, depth, line, depth, (gz, (1 - y) * 2 + core)).wait_send()
        spill_copy(depth + 1, depth + 1, pair, 2 * depth, (z * 2 + 1 - x, gy)).wait_send()
        spill_copy(depth + 2, depth + 2, half, 4 * depth, (gz, y * 2 + 1 - core)).wait_send()

    for s in range(SWEEPS):
        for side in range(2):
            a = PAD if side == 0 else cols
            pl.when((gz > 0, gz < n_gz - 1)[side])(
                lambda s=s, side=side: pltpu.make_async_remote_copy(
                    src_ref=z_send.at[s, side],
                    dst_ref=z_recv.at[s, 1 - side],
                    send_sem=z_sems.at[s, 0, side],
                    recv_sem=z_sems.at[s, 1, 1 - side],
                    device_id=(gz - 1 + 2 * side, gy),
                    device_id_type=MESH,
                ).wait_send()
            )
            pl.when((gy > 0, gy < n_gy - 1)[side])(
                lambda s=s, side=side, a=a: pltpu.make_async_remote_copy(
                    src_ref=ext.at[s, :, body_rows, pl.ds(a, PAD)],
                    dst_ref=ext.at[s, :, body_rows, pl.ds(a, PAD)],
                    send_sem=y_sems.at[s, 0, side],
                    recv_sem=y_sems.at[s, 1, 1 - side],
                    device_id=(gz, gy - 1 + 2 * side),
                    device_id_type=MESH,
                ).wait_send()
            )

    def told(i, carry):
        o = partner(i, n, me)
        note_copy(o, o).wait()
        return carry

    lax.fori_loop(0, n - 1, told, 0)

    if lean:
        own_copy.wait()

        def finish(i, carry):
            o = partner(i, n, me)
            row_copy(o, o).wait()
            return carry

        lax.fori_loop(0, n - 1, finish, 0)


def send_dense(
    n_gz, n_gy, cap, blocks, index, solid, got, send, out_sems, in_sems, own_sem
):
    n = n_gz * n_gy
    cp = padded_rows(cap + 1)
    me = lax.axis_index("gz") * n_gy + lax.axis_index("gy")
    greet_all(n, n_gy, me)

    def row_copy(o, at):
        return pltpu.make_async_remote_copy(
            src_ref=send.at[o],
            dst_ref=got.at[at],
            send_sem=out_sems.at[o],
            recv_sem=in_sems.at[at],
            device_id=(o // n_gy, lax.rem(o, n_gy)),
            device_id_type=MESH,
        )

    def fill(o):
        for l in range(cap):
            k = index[o * cap + l]
            send[o, l : l + 1, :] = blocks[0, pl.ds(k, 1), :]
            send[o, cp + l : cp + l + 1, :] = blocks[1, pl.ds(k, 1), :]
        send[o, cap : cap + 1, :] = solid[pl.ds(o, 1), :]

    def push(i, carry):
        o = partner(i, n, me)
        fill(o)
        row_copy(o, me).start()
        return carry

    lax.fori_loop(0, n - 1, push, 0)
    fill(me)
    own_copy = pltpu.make_async_copy(send.at[me], got.at[me], own_sem)
    own_copy.start()
    own_copy.wait()

    def finish(i, carry):
        o = partner(i, n, me)
        row_copy(o, o).wait()
        return carry

    lax.fori_loop(0, n - 1, finish, 0)


def creep(cap, got, chain, micro, chain_out, micro_out, change):
    cp = padded_rows(cap + 1)
    unit = lax.broadcasted_iota(jnp.int32, (KU, SITES), 0)
    speed = jnp.full((KU, SITES), -10.0, jnp.float32)
    for m in range(1, KU):
        speed = jnp.where(unit == m, -10.0 / 3.0**m, speed)
    sub = lax.broadcasted_iota(jnp.int32, (cap, SITES), 0)
    lane = lax.broadcasted_iota(jnp.int32, (cap, SITES), 1)
    for q in range(GROUP):
        base = q * cap
        phi = got[q, 0:cap, :]
        stress = got[q, cp : cp + cap, :]
        row = got[q, cap : cap + 1, :]
        solid = jnp.sum(jnp.where(sub == lane, row, 0.0), axis=1, keepdims=True)
        s0 = micro[base : base + cap, :]
        s1 = s0 / (1.0 + 0.2 * phi * s0)
        micro_out[base : base + cap, :] = s1
        flow = 0.1 * phi * s1 * stress
        for l0 in range(0, cap, 8):
            l1 = min(l0 + 8, cap)
            old = chain[base + l0 : base + l1]
            decay = jnp.exp(phi[l0:l1][:, None, :] * speed[None])
            new = decay * old + 0.15 * (1.0 - decay) * stress[l0:l1][:, None, :]
            chain_out[base + l0 : base + l1] = new
            kelvin = jnp.sum(new - old, axis=1)
            change[q, l0:l1, :] = solid[l0:l1] * kelvin + flow[l0:l1]
        change[q, cap:cp, :] = jnp.zeros((cp - cap, SITES), jnp.float32)


def creep_and_return(
    n_gz, n_gy, cap,
    got, spill, notes, micro, where, chain,
    out, micro_out, chain_out,
    old_state, new_state, change, back, read_sems, write_sems, out_sems, in_sems,
):
    n = n_gz * n_gy
    depth = n // 8
    rows, cols = out.shape
    gz = lax.axis_index("gz")
    gy = lax.axis_index("gy")
    me = gz * n_gy + gy
    held = DIRECT + SPILL
    part = n_gy * cap

    def read(g):
        at = pl.ds(g * part, part)
        return pltpu.make_async_copy(chain.at[at], old_state.at[at], read_sems.at[g])

    def write(g):
        at = pl.ds(g * part, part)
        return pltpu.make_async_copy(new_state.at[at], chain_out.at[at], write_sems.at[g])

    def turn(i):
        mid = n_gz // 2
        return lax.rem(gz // mid + 1 + i // mid, 2) * mid + lax.rem(gz + i, mid)

    def begin(i, carry):
        read(turn(i)).start()
        return carry

    lax.fori_loop(0, n_gz, begin, 0)
    greet_all(n, n_gy, me)

    unit = lax.broadcasted_iota(jnp.int32, (KU, SITES), 0)
    speed = jnp.full((KU, SITES), -10.0, jnp.float32)
    for m in range(1, KU):
        speed = jnp.where(unit == m, -10.0 / 3.0**m, speed)
    tall = -(-cap // 16) * 16
    sub = lax.broadcasted_iota(jnp.int32, (tall, SITES), 0)
    lane = lax.broadcasted_iota(jnp.int32, (tall, SITES), 1)
    row_id = lax.rem(lax.broadcasted_iota(jnp.int32, (tall, 3 * held), 1), held)
    row_id = row_id.astype(jnp.float32)

    def row_copy(o, at):
        return pltpu.make_async_remote_copy(
            src_ref=change.at[o],
            dst_ref=back.at[at],
            send_sem=out_sems.at[o],
            recv_sem=in_sems.at[at],
            device_id=(o // n_gy, lax.rem(o, n_gy)),
            device_id_type=MESH,
        )

    def group(i, carry):
        g = turn(i)
        read(g).wait()
        start = pl.multiple_of(g * part, 8)
        s0 = micro[pl.ds(start, part), :]
        z, x = g // 2, lax.rem(g, 2)
        all_phi = []
        all_stress = []
        all_solid = []
        for q in range(n_gy):
            o = g * n_gy + q
            place = (q % 2 * 4 + x * 2 + q // 2) * depth + z

            def column(r):
                row = notes[o, r : r + 1, :]
                return jnp.sum(jnp.where(sub == lane, row, 0.0), axis=1, keepdims=True)

            pick = jnp.where(column(0) == row_id, 1.0, 0.0).astype(jnp.bfloat16)
            all_solid.append(column(1)[:cap])
            rows_phi = jnp.concatenate([got[o, 0:DIRECT, :], spill[place, 0:SPILL, :]], axis=0)
            rows_stress = jnp.concatenate(
                [got[o, DIRECT : 2 * DIRECT, :], spill[place, SPILL : 2 * SPILL, :]], axis=0
            )
            both = jnp.concatenate([rows_phi, rows_stress], axis=1)
            high = both.astype(jnp.bfloat16)
            left = both - high.astype(jnp.float32)
            middle = left.astype(jnp.bfloat16)
            low = (left - middle.astype(jnp.float32)).astype(jnp.bfloat16)
            parts = jnp.concatenate([high, middle, low], axis=0)
            both = jnp.dot(pick, parts, preferred_element_type=jnp.float32)
            all_phi.append(both[:cap, :SITES])
            all_stress.append(both[:cap, SITES:])
        phis = jnp.concatenate(all_phi, axis=0)
        s1 = s0 / (1.0 + 0.2 * phis * s0)
        micro_out[pl.ds(start, part), :] = s1
        for q in range(n_gy):
            o = g * n_gy + q
            phi, stress, solid = all_phi[q], all_stress[q], all_solid[q]
            flow = 0.1 * phi * s1[q * cap : (q + 1) * cap] * stress
            base = g * part + q * cap
            for l0 in range(0, cap, 8):
                l1 = min(l0 + 8, cap)
                at = pl.ds(base + l0, l1 - l0)
                old = old_state[at]
                decay = jnp.exp(phi[l0:l1][:, None, :] * speed[None])
                new = decay * old + 0.15 * (1.0 - decay) * stress[l0:l1][:, None, :]
                new_state[at] = new
                kelvin = jnp.sum(new - old, axis=1)
                change[o, l0:l1, :] = solid[l0:l1] * kelvin + flow[l0:l1]
            pl.when(o != me)(lambda o=o: row_copy(o, me).start())
        write(g).start()
        return carry

    lax.fori_loop(0, n_gz, group, 0)
    back[me] = change[me]

    def finish(i, carry):
        o = partner(i, n, me)
        row_copy(o, o).wait()
        return carry

    lax.fori_loop(0, n - 1, finish, 0)
    per_row = cols // SITES

    def place_cells(g, carry):
        r = pl.multiple_of(g * 8, 8)
        for j in range(per_row):
            lines = []
            for k in range(8):
                w = where[j * rows + r + k]
                lines.append(back[w // 256, pl.ds(lax.rem(w, 256), 1), :])
            out[pl.ds(r, 8), j * SITES : (j + 1) * SITES] = jnp.concatenate(lines, axis=0)
        return carry

    lax.fori_loop(0, rows // 8, place_cells, 0)

    def end(i, carry):
        write(turn(i)).wait()
        return carry

    lax.fori_loop(0, n_gz, end, 0)


def send_back(n_gz, n_gy, change, where, out, back, out_sems, in_sems):
    n = n_gz * n_gy
    rows, cols = out.shape
    cp = change.shape[1]
    me = lax.axis_index("gz") * n_gy + lax.axis_index("gy")
    greet_all(n, n_gy, me)

    def push(i, carry):
        o = partner(i, n, me)
        pltpu.make_async_remote_copy(
            src_ref=change.at[o],
            dst_ref=back.at[pl.ds(pl.multiple_of(me * cp, 8), cp)],
            send_sem=out_sems.at[o],
            recv_sem=in_sems.at[me],
            device_id=(o // n_gy, lax.rem(o, n_gy)),
            device_id_type=MESH,
        ).start()
        return carry

    lax.fori_loop(0, n - 1, push, 0)
    back[pl.ds(pl.multiple_of(me * cp, 8), cp), :] = change[me]

    def finish(i, carry):
        o = partner(i, n, me)
        pltpu.make_async_remote_copy(
            src_ref=change.at[o],
            dst_ref=back.at[pl.ds(pl.multiple_of(o * cp, 8), cp)],
            send_sem=out_sems.at[o],
            recv_sem=in_sems.at[o],
            device_id=(o // n_gy, lax.rem(o, n_gy)),
            device_id_type=MESH,
        ).wait()
        return carry

    lax.fori_loop(0, n - 1, finish, 0)
    per_row = cols // SITES

    def place(g, carry):
        r = pl.multiple_of(g * 8, 8)
        for j in range(per_row):
            lines = [back[pl.ds(where[j * rows + r + k], 1), :] for k in range(8)]
            out[pl.ds(r, 8), j * SITES : (j + 1) * SITES] = jnp.concatenate(lines, axis=0)
        return carry

    lax.fori_loop(0, rows // 8, place, 0)


def body(n_gz, n_gy, warmth, moisture, degree, tally, keeper, pouring, chain, micro):
    n = n_gz * n_gy
    rows, cols = warmth.shape
    per_row = cols // SITES
    slots = chain.shape[0]
    cap = slots // n
    cp = padded_rows(cap + 1)
    nb = rows * per_row
    lifts = rows // LIFT
    vm = pl.BlockSpec(memory_space=pltpu.VMEM)
    sm = pl.BlockSpec(memory_space=pltpu.SMEM)
    hbm = pl.BlockSpec(memory_space=pl.ANY)
    far = pl.BlockSpec(memory_space=pltpu.HBM)
    f32 = jnp.float32

    local_times = lax.dynamic_slice_in_dim(pouring, lax.axis_index("gz") * lifts, lifts)
    age = 2400.0 - jnp.repeat(local_times, LIFT).astype(f32)
    solid = jnp.sqrt(600.0 / age) + 0.2
    flat = keeper.T.reshape(-1)
    slot_id = jnp.arange(slots, dtype=jnp.int32)
    hit = flat[None, :] == slot_id[:, None]
    block = jnp.arange(nb, dtype=jnp.int32)
    solid_slot = jnp.sum(jnp.where(hit, jnp.tile(solid, per_row)[None, :], 0.0), axis=1)
    solid_rows = jnp.pad(solid_slot.reshape(n, cap), ((0, 0), (0, SITES - cap)))
    lean = cap >= DIRECT + 8 and n % 8 == 0 and n_gy == 4 and GROUP * cap % 8 == 0
    owner = flat // cap
    earlier = flat[None, :] < flat[:, None]
    if lean:
        rank = jnp.sum(earlier & (owner[None, :] == owner[:, None]), axis=1, dtype=jnp.int32)
        over = rank >= DIRECT
        spot = jnp.sum(earlier & over[None, :], axis=1, dtype=jnp.int32)
        spilled = jnp.sum(over, dtype=jnp.int32)
        code = jnp.where(over, DIRECT + spot, rank)
        slot_map = jnp.sum(jnp.where(hit, code[None, :] + 1, 0), axis=1) - 1
        target = jnp.where(over, n * DIRECT + spot, owner * DIRECT + rank)
        line_id = jnp.arange(n * DIRECT + SPILL, dtype=jnp.int32)
        fits = target[None, :] == line_id[:, None]
        index = nb + jnp.sum(jnp.where(fits, block[None, :] - nb, 0), axis=1)
        slot_map = jnp.pad(slot_map.reshape(n, cap).astype(f32), ((0, 0), (0, SITES - cap)))
        count = jnp.broadcast_to(spilled.astype(f32), (n, SITES))
        notes = [slot_map, solid_rows, count]
    else:
        index = jnp.zeros((8,), jnp.int32)
        notes = [solid_rows, solid_rows, solid_rows]
    notes = jnp.stack(notes + [jnp.zeros((n, SITES), f32)] * 5, axis=1)

    field = jax.ShapeDtypeStruct((rows, cols), f32)
    outs = [field, field, field, jax.ShapeDtypeStruct((2, nb + 8, SITES), f32)]
    outs += [jax.ShapeDtypeStruct((n, 8, SITES), f32)]
    scratch = [
        pltpu.VMEM((SWEEPS, 2, rows + 2 * TOP, cols + 2 * PAD), f32),
        pltpu.VMEM((rows + 2 * TOP, cols + 2 * PAD), f32),
        pltpu.VMEM((SWEEPS, 2, 2, cols), f32),
        pltpu.VMEM((SWEEPS, 2, 2, cols), f32),
        pltpu.SemaphoreType.DMA((SWEEPS, 2, 2)),
        pltpu.SemaphoreType.DMA((SWEEPS, 2, 2)),
        pltpu.SemaphoreType.DMA((n,)),
        pltpu.SemaphoreType.DMA((n,)),
        pltpu.VMEM((rows, cols), f32),
        pltpu.VMEM((rows, per_row), jnp.int32),
        pltpu.SemaphoreType.DMA((4,)),
    ]
    out_specs = [vm] * 5
    if lean:
        outs += [jax.ShapeDtypeStruct((n, 2 * DIRECT, SITES), f32)]
        outs += [jax.ShapeDtypeStruct((n, 2 * SPILL, SITES), f32)]
        out_specs += [hbm, vm]
        scratch += [
            pltpu.VMEM((n, 2 * DIRECT, SITES), f32),
            pltpu.SemaphoreType.DMA((n,)),
            pltpu.SemaphoreType.DMA((n,)),
            pltpu.SemaphoreType.DMA,
            pltpu.SemaphoreType.DMA((n // 8 + 3,)),
            pltpu.SemaphoreType.DMA((n // 8 + 3,)),
        ]
    limit = 40 * 1024 * 1024
    results = pl.pallas_call(
        functools.partial(sweep_and_send, n_gz, n_gy, lean),
        out_shape=tuple(outs),
        in_specs=[far, far, far, far, sm, vm],
        out_specs=tuple(out_specs),
        scratch_shapes=scratch,
        compiler_params=pltpu.CompilerParams(
            collective_id=0, has_side_effects=True, vmem_limit_bytes=60 * 1024 * 1024
        ),
        name="sweep_and_send",
    )(warmth, moisture, degree, tally, index, notes)
    temp, hum, degree_after, blocks, notes_in = results[:5]

    state_specs = (
        pl.BlockSpec((GROUP * cap, KU, SITES), lambda i: (i, 0, 0)),
        pl.BlockSpec((GROUP * cap, SITES), lambda i: (i, 0)),
    )
    state_shapes = (
        jax.ShapeDtypeStruct(chain.shape, f32),
        jax.ShapeDtypeStruct(micro.shape, f32),
    )

    def dense_tail(*_):
        held_there = flat[None, :] == slot_id[:, None]
        index = nb + jnp.sum(jnp.where(held_there, block[None, :] - nb, 0), axis=1)
        where = (flat // cap) * cp + flat % cap
        got = pl.pallas_call(
            functools.partial(send_dense, n_gz, n_gy, cap),
            out_shape=jax.ShapeDtypeStruct((n, 2 * cp, SITES), f32),
            in_specs=[vm, sm, vm],
            out_specs=hbm,
            scratch_shapes=[
                pltpu.VMEM((n, 2 * cp, SITES), f32),
                pltpu.SemaphoreType.DMA((n,)),
                pltpu.SemaphoreType.DMA((n,)),
                pltpu.SemaphoreType.DMA,
            ],
            compiler_params=pltpu.CompilerParams(
                collective_id=2, has_side_effects=True, vmem_limit_bytes=limit
            ),
            name="send_dense",
        )(blocks, index, solid_rows)
        chain_after, micro_after, change = pl.pallas_call(
            functools.partial(creep, cap),
            grid=(n // GROUP,),
            out_shape=state_shapes + (jax.ShapeDtypeStruct((n, cp, SITES), f32),),
            in_specs=[pl.BlockSpec((GROUP, 2 * cp, SITES), lambda i: (i, 0, 0)), *state_specs],
            out_specs=(*state_specs, pl.BlockSpec((GROUP, cp, SITES), lambda i: (i, 0, 0))),
            compiler_params=pltpu.CompilerParams(vmem_limit_bytes=limit),
            name="creep",
        )(got, chain, micro)
        cells = pl.pallas_call(
            functools.partial(send_back, n_gz, n_gy),
            out_shape=field,
            in_specs=[vm, sm],
            out_specs=vm,
            scratch_shapes=[
                pltpu.VMEM((n * cp, SITES), f32),
                pltpu.SemaphoreType.DMA((n,)),
                pltpu.SemaphoreType.DMA((n,)),
            ],
            compiler_params=pltpu.CompilerParams(
                collective_id=1, has_side_effects=True, vmem_limit_bytes=limit
            ),
            name="send_back",
        )(change, where)
        return cells, chain_after, micro_after

    def lean_tail(got, got_spill):
        where = owner * 256 + flat % cap
        cells, micro_after, chain_after = pl.pallas_call(
            functools.partial(creep_and_return, n_gz, n_gy, cap),
            out_shape=(field, state_shapes[1], state_shapes[0]),
            in_specs=[vm, vm, vm, vm, sm, hbm],
            out_specs=(vm, vm, hbm),
            scratch_shapes=[
                pltpu.VMEM(chain.shape, f32),
                pltpu.VMEM(chain.shape, f32),
                pltpu.VMEM((n, cap, SITES), f32),
                pltpu.VMEM((n, cap, SITES), f32),
                pltpu.SemaphoreType.DMA((n_gz,)),
                pltpu.SemaphoreType.DMA((n_gz,)),
                pltpu.SemaphoreType.DMA((n,)),
                pltpu.SemaphoreType.DMA((n,)),
            ],
            compiler_params=pltpu.CompilerParams(
                collective_id=3, has_side_effects=True, vmem_limit_bytes=limit
            ),
            name="creep_and_return",
        )(got, got_spill, notes_in, micro, where, chain)
        return cells, chain_after, micro_after

    if lean:
        fits_all = jnp.max(notes_in[:, 2, 0]) <= SPILL
        creep_cells, chain_after, micro_after = lax.cond(
            fits_all, lean_tail, dense_tail, *results[5:]
        )
    else:
        creep_cells, chain_after, micro_after = dense_tail()
    return temp, hum, degree_after, creep_cells, chain_after, micro_after


def solution(mesh):
    n_gz, n_gy = mesh.shape["gz"], mesh.shape["gy"]
    cells = P("gz", "gy")
    states = P(("gz", "gy"), None, None)
    tension = P(("gz", "gy"), None)
    return jax.shard_map(
        functools.partial(body, n_gz, n_gy),
        mesh=mesh,
        in_specs=(cells, cells, cells, cells, cells, P(), states, tension),
        out_specs=(cells, cells, cells, cells, states, tension),
        check_vma=False,
    )
```
